512 devices in a mesh: mem: 16 (over y, z_hi), tt: 32 (over x, z_lo, core).
Axes of the slice: x: 4, y: 4, z: 16 (z_hi: 4, z_lo: 4; z = z_hi * 4 + z_lo), core: 2. Of those that a mesh axis runs over, the one named last changes fastest.
Arguments:
- history: bfloat16 [2, 64, 128, 64, 128], P(None, 'mem', None, 'tt'), may hold values from -0.0625 to 0.0625
- free_rows: bfloat16 [2, 2, 128, 64, 128], P(None, None, None, 'tt'), may hold values from -3 to 3
- memory_start: int32 [2], replicated, may hold values from 0 to 31, as said below
- now: int32 [1], replicated, may hold values from 32 to 62
Outputs:
- new_rows: bfloat16 [2, 2, 128, 64, 128], P(None, None, None, 'tt')
The draws below stay inside these ranges and needn't reach their ends.
Inputs may be any that keep to these rules, and one draw needn't show every extreme that they name: Row r's memory integral starts at memory_start[r]; starts need not be distinct, and some row starts at the largest allowed value. The new rows' times now + r lie inside the grid.
All inputs are finite; a program needn't handle non-finite values.
Results may differ from the reference program's by a relative error of at most 0.012.
The reference program's roundings to bfloat16 on the way count: a program that leaves them out, or rounds other values in their place, can miss the bound.
Values may be sent and summed in bfloat16 or wider, within the bound.
A program may use at most 64 MiB of HBM per device.

```python
import jax
import jax.numpy as jnp

NORB = 128
ROWS = 2
ITERS = 3
NT = 64


def draw_memory_start(key, part):
    half = NT // 2
    value_key = jax.random.fold_in(key, 11)
    place_key = jax.random.fold_in(key, 23)
    values = jax.random.randint(value_key, (ROWS,), 0, half, dtype=jnp.int32)
    chosen = jax.random.randint(place_key, (), 0, ROWS, dtype=jnp.int32)
    positions = jnp.arange(ROWS, dtype=jnp.int32)
    values = jnp.where(positions == chosen, jnp.int32(half - 1), values)
    return values.astype(jnp.int32)


def block_scale(stream_key, extent, split, least, top_value):
    loudness, own = 1.0, jax.random.fold_in(stream_key, 6)
    for axis_at, parts in split:
        heights = jnp.exp(jax.random.uniform(jax.random.fold_in(own, axis_at), (parts,), jnp.float32, least / len(split), top_value / len(split)))
        loudness = loudness * jnp.repeat(heights, extent[axis_at] // parts).reshape([-1 if axis == axis_at else 1 for axis in range(len(extent))])
    return loudness


def normal_values(key, dims, scale, bound, split=(), held_as=jnp.bfloat16):
    array = scale * jax.random.normal(key, dims, jnp.float32)
    if split:
        array = array * block_scale(key, dims, split, -0.22, 0.18)
    return jnp.clip(array, -bound, bound).astype(held_as)


def setup_inputs(seed: int = 0) -> dict:
    seeds = jax.random.split(jax.random.key(seed), 5)
    return {
        "history": normal_values(seeds[0], (2, NT, NORB, NT, NORB), (NT * NORB) ** -0.5, 0.0625, ((1, 16), (3, 32))),
        "free_rows": normal_values(seeds[1], (2, ROWS, NORB, NT, NORB), 0.5, 3.0, ((3, 32),)),
        "memory_start": draw_memory_start(jax.random.fold_in(seeds[4], 71), 0),
        "now": jax.random.randint(seeds[3], (1,), NT // 2, NT - ROWS + 1).astype(jnp.int32),
    }


COUPLING = 0.5


def reference(history, free_rows, memory_start, now):
    hist_real = history[0].reshape(NT * NORB, NT * NORB)
    hist_imag = history[1].reshape(NT * NORB, NT * NORB)
    mem_times = jnp.arange(NT, dtype=jnp.int32)
    row_time = now[0] + jnp.arange(ROWS, dtype=jnp.int32)
    live_mask = (mem_times[None, :] >= memory_start[:, None]) & (mem_times[None, :] < row_time[:, None])
    live_weight = live_mask.astype(jnp.float32)[:, None, :, None]
    free_flat = free_rows.astype(jnp.float32).reshape(2, ROWS * NORB, NT * NORB)
    current = free_rows
    for sweep in range(ITERS):
        real_part = current[0].astype(jnp.float32)
        imag_part = current[1].astype(jnp.float32)
        modulus = real_part * real_part + imag_part * imag_part
        sig_real = (-(real_part * modulus) * live_weight).astype(jnp.bfloat16).reshape(ROWS * NORB, NT * NORB)
        sig_imag = (-(imag_part * modulus) * live_weight).astype(jnp.bfloat16).reshape(ROWS * NORB, NT * NORB)
        out_real = jnp.dot(sig_real, hist_real, preferred_element_type=jnp.float32) - jnp.dot(sig_imag, hist_imag, preferred_element_type=jnp.float32)
        out_imag = jnp.dot(sig_real, hist_imag, preferred_element_type=jnp.float32) + jnp.dot(sig_imag, hist_real, preferred_element_type=jnp.float32)
        summed = jnp.stack([out_real, out_imag])
        current = (free_flat + COUPLING * summed).astype(jnp.bfloat16).reshape(free_rows.shape)
    return current
```

```python
import functools

import jax
import jax.numpy as jnp
from jax import lax
from jax.experimental import pallas as pl
from jax.experimental.pallas import tpu as pltpu
from jax.sharding import PartitionSpec as P

ITERS = 3
COUPLING = 0.5
MESH = pl.DeviceIdType.MESH
BF16 = jnp.bfloat16
F32 = jnp.float32


def device(x, y, zh, zl, c):
    return (y * 4 + zh, x * 8 + zl * 2 + c)


def kernel(
    hist, free, start, now, out,
    hraw, htmp, h_all, fraw, ftmp, fpc, fa, fb, gsend, grecv, rsend, rrecv, xfin, pieces, otmp,
    lsem, hy_s, hy_r, hs_s, hs_r, f_s, f_r, g_s, g_r, r_s, r_r, az_s, az_r, ay_s, ay_r,
):
    mem, tt = lax.axis_index("mem"), lax.axis_index("tt")
    y, zh = mem // 4, mem % 4
    x, zl, c = tt // 8, (tt // 2) % 4, tt % 2
    sib = device(x, y, zh, zl, 1 - c)

    def remote(src, dst, ssem, rsem, dev):
        return pltpu.make_async_remote_copy(
            src_ref=src, dst_ref=dst, send_sem=ssem, recv_sem=rsem, device_id=dev, device_id_type=MESH
        )

    load_h = pltpu.make_async_copy(hist, hraw, lsem.at[0])
    load_f = pltpu.make_async_copy(free, fraw, lsem.at[1])
    load_h.start()
    load_f.start()

    barrier = pltpu.get_barrier_semaphore()
    partners = []
    for dz in range(16):
        z = (zh * 4 + zl + dz) % 16
        for dc in range(2):
            if dz or dc:
                partners.append(device(x, y, z // 4, z % 4, (c + dc) % 2))
    for dx in range(1, 4):
        for dz in range(4):
            partners.append(device((x + dx) % 4, y, zh, (zl + dz) % 4, c))
    for dy in range(1, 4):
        partners.append(device(x, (y + dy) % 4, zh, zl, c))
    for dev in partners:
        pl.semaphore_signal(barrier, inc=1, device_id=dev, device_id_type=MESH)

    load_f.wait()
    for part in range(2):
        for r in range(2):
            rows = pl.ds(pl.multiple_of(y * 64, 64), 64)
            ftmp[part, r] = fraw[part, r, rows, :].astype(F32)
    for part in range(2):
        for r in range(2):
            for t in range(2):
                fpc[t, r, part * 32 : part * 32 + 32, :] = ftmp[part, r, pl.ds(t, 32, stride=2), :].astype(BF16)

    load_h.wait()
    for sl in range(4):
        for part in range(2):
            htmp[sl, part] = hraw[part, sl].astype(F32)
        for part in range(2):
            for t in range(2):
                col = (t * 2 + part) * 128
                h_all[y, c, sl * 128 : sl * 128 + 128, col : col + 128] = htmp[
                    sl, part, pl.ds(t, 128, stride=2), :
                ].astype(BF16)

    pl.semaphore_wait(barrier, len(partners))
    sends = []

    for t in range(2):
        for r in range(2):
            to = 2 * c + t
            mine = (zl == to) & (c == r)

            @pl.when((zl == zh) & mine)
            def _():
                fa[...] = fpc[t, r]

            @pl.when((zl == zh) & jnp.logical_not(mine))
            def _():
                remote(fpc.at[t, r], fa, f_s.at[t * 2 + r], f_r.at[0], device(x, y, zh, to, r)).start()

    @pl.when(c == zh // 2)
    def _():
        fb[...] = fpc[zh % 2, c]
        remote(fpc.at[zh % 2, 1 - c], fb, f_s.at[4], f_r.at[1], sib).start()

    up, down, far = (y + 1) % 4, (y + 3) % 4, (y + 2) % 4
    up_dev, down_dev = device(x, up, zh, zl, c), device(x, down, zh, zl, c)

    def slab(b, core, sl):
        return h_all.at[b, core, pl.ds(sl * 128, 128), :]

    def hy(b, sl, k, dev):
        cp = remote(slab(b, c, sl), slab(b, c, sl), hy_s.at[k], hy_r.at[k], dev)
        cp.start()
        sends.append(cp)

    def hs(b, sl, k):
        cp = remote(slab(b, c, sl), slab(b, c, sl), hs_s.at[k], hs_r.at[k], sib)
        cp.start()
        sends.append(cp)

    def hy_wait(b, sl, k):
        remote(slab(b, c, sl), slab(b, c, sl), hy_s.at[k], hy_r.at[k], up_dev).wait_recv()

    for k in range(4):
        hy(y, k, k, up_dev)
        hy(y, (k + 2) % 4, 4 + k, down_dev)
    for k in range(4):
        hs(y, k, k)

    @pl.when(jnp.logical_not((zl == zh) & (c == zl // 2)))
    def _():
        remote(fpc.at[0, 0], fa, f_s.at[0], f_r.at[0], sib).wait_recv()

    s_time = 16 * x + 4 * zh + zl
    live = jnp.where((start[c] <= s_time) & (s_time < now[0] + c), 1.0, 0.0).astype(F32)

    def gather(n, value):
        re, im = value[:32].astype(F32), value[32:].astype(F32)
        mod = re * re + im * im
        gsend[n, :32, :] = (-(re * mod) * live).astype(BF16)
        gsend[n, 32:, :] = (-(im * mod) * live).astype(BF16)
        for dx, dz in G_ORDER:
            dev = device((x + dx) % 4, y, zh, (zl + dz) % 4, c)
            cp = remote(gsend.at[n], grecv.at[n, x, zl], g_s.at[n, dx * 4 + dz], g_r.at[n, x, zl], dev)
            cp.start()
            sends.append(cp)
        grecv[n, x, zl] = gsend[n]

    def g_wait(n, dx):
        for dz in range(4):
            if dx or dz:
                b = grecv.at[n, (x + dx) % 4, (zl + dz) % 4]
                remote(b, b, g_s.at[n, 0], g_r.at[n, (x + dx) % 4, (zl + dz) % 4], sib).wait_recv()

    def multiply(n, order, wait):
        acc = [None, None]
        for d in order:
            if wait:
                g_wait(n, d)
            b = (x + d) % 4 if wait else (y + d) % 4
            left = jnp.concatenate([grecv[n, b, sl] for sl in range(4)], axis=1)
            for core in range(2):
                prod = jnp.dot(left, h_all[b, core], preferred_element_type=F32)
                acc[core] = prod if acc[core] is None else acc[core] + prod
        for t in range(4):
            p = acc[t // 2][:, (t % 2) * 256 : (t % 2) * 256 + 256]
            rsend[n, t, :32, :] = (p[:32, :128] - p[32:, 128:]).astype(BF16)
            rsend[n, t, 32:, :] = (p[:32, 128:] + p[32:, :128]).astype(BF16)

    def r_send(n, last):
        for t in range(4):
            if last:
                here, dev = zh == t, device(x, y, t, zl, c)
            else:
                here, dev = (zh == zl) & (zl == t), device(x, y, zl, t, c)

            @pl.when(here)
            def _():
                rrecv[n, zh] = rsend[n, t]

            @pl.when(jnp.logical_not(here))
            def _():
                remote(rsend.at[n, t], rrecv.at[n, zh], r_s.at[n, t], r_r.at[n, zh], dev).start()

    def r_each(n, last, do):
        for t in range(4):
            here = (zh == t) if last else (zh == zl) & (zl == t)
            pl.when(jnp.logical_not(here))(functools.partial(do, t))

    def r_sum(n, last, base):
        for src in range(4):
            here = (zh == src) if last else (zh == zl) & (zh == src)

            @pl.when(jnp.logical_not(here))
            def _():
                remote(rrecv.at[n, src], rrecv.at[n, src], r_s.at[n, src], r_r.at[n, src], sib).wait_recv()

        total = rrecv[n, 0].astype(F32) + rrecv[n, 1].astype(F32) + rrecv[n, 2].astype(F32) + rrecv[n, 3].astype(F32)
        return (base[...].astype(F32) + COUPLING * total).astype(BF16)

    gather(0, fa[...])

    for k in range(4):
        hy_wait(down, k, k)
        if k < 2:
            hy(down, k, 8 + k, up_dev)
        hs(down, k, 4 + k)
        sl = (k + 2) % 4
        hy_wait(up, sl, 4 + k)
        if k < 2:
            hy(up, sl, 10 + k, down_dev)
        hs(up, sl, 8 + k)
    for k in range(2):
        hy_wait(far, k, 8 + k)
        hs(far, k, 12 + k)
        hy_wait(far, k + 2, 10 + k)
        hs(far, k + 2, 14 + k)
    for d in range(4):
        g_wait(0, d)
    for b, ks in ((y, ((0, 0), (1, 1), (2, 2), (3, 3))), (down, ((0, 4), (1, 5), (2, 6), (3, 7))),
                  (up, ((2, 8), (3, 9), (0, 10), (1, 11))), (far, ((0, 12), (1, 13), (2, 14), (3, 15)))):
        for sl, k in ks:
            remote(slab(b, 1 - c, sl), slab(b, 1 - c, sl), hs_s.at[k], hs_r.at[k], sib).wait_recv()

    for n in range(ITERS):
        last = n == ITERS - 1
        multiply(n, (0, 1, 3, 2), n > 0)
        r_send(n, last)
        if not last:
            gather(n + 1, r_sum(n, last, fa))

    @pl.when(c != zh // 2)
    def _():
        remote(fpc.at[0, 0], fb, f_s.at[4], f_r.at[1], sib).wait_recv()

    xfin[...] = r_sum(ITERS - 1, True, fb)

    core = zh // 2
    for d in (2, 1, 3, 0):
        dev = device(x, y, (zh + d) % 4, zl, core)

        def go(d=d, dev=dev):
            remote(xfin, pieces.at[y, zh % 2, c], az_s.at[d], az_r.at[zh % 2, c], dev).start()

        if d:
            go()
        else:
            @pl.when(core != c)
            def _():
                go()

            @pl.when(core == c)
            def _():
                pieces[y, zh % 2, c] = xfin[...]

    near = jnp.where((zh == 2 * c) | (zh == (2 * c + 3) % 4), 0, 1)
    for order in range(2):
        t = near if order == 0 else 1 - near
        for r in range(2):
            src = pieces.at[y, t, r]

            @pl.when(jnp.logical_not((zh == 2 * c + t) & (c == r)))
            def _():
                remote(src, src, az_s.at[0], az_r.at[t, r], sib).wait_recv()

            for dy in (2, 1, 3):
                k = (dy - 1) * 4 + order * 2 + r
                cp = remote(src, src, ay_s.at[k], ay_r.at[y, t, r], device(x, (y + dy) % 4, zh, zl, c))
                cp.start()
                sends.append(cp)

    def assemble(b):
        for t in range(2):
            for r in range(2):
                for part in range(2):
                    otmp[part, r, pl.ds(pl.multiple_of(b * 64, 64) + t, 32, stride=2), :] = pieces[
                        b, t, r, part * 32 : part * 32 + 32, :
                    ].astype(F32)
        for r in range(2):
            for part in range(2):
                rows = pl.ds(pl.multiple_of(b * 64, 64), 64)
                out[part, r, rows, :] = otmp[part, r, rows, :].astype(BF16)

    assemble(y)
    for dy in (1, 3, 2):
        b = (y + dy) % 4
        for t in range(2):
            for r in range(2):
                remote(pieces.at[b, t, r], pieces.at[b, t, r], ay_s.at[0], ay_r.at[b, t, r], sib).wait_recv()
        assemble(b)

    for t in range(2):
        for r in range(2):
            @pl.when((zl == zh) & jnp.logical_not((zl == 2 * c + t) & (c == r)))
            def _():
                remote(fpc.at[t, r], fa, f_s.at[t * 2 + r], f_r.at[0], sib).wait_send()

    @pl.when(c == zh // 2)
    def _():
        remote(fpc.at[0, 0], fb, f_s.at[4], f_r.at[1], sib).wait_send()

    for n in range(ITERS):
        r_each(n, n == ITERS - 1, lambda t, n=n: remote(
            rsend.at[n, t], rrecv.at[n, t], r_s.at[n, t], r_r.at[n, t], sib).wait_send())
    for d in range(4):
        def done(d=d):
            remote(xfin, pieces.at[0, 0, 0], az_s.at[d], az_r.at[0, 0], sib).wait_send()

        if d:
            done()
        else:
            pl.when(core != c)(done)
    for cp in sends:
        cp.wait_send()


G_ORDER = tuple(
    sorted(
        ((dx, dz) for dx in range(4) for dz in range(4) if dx or dz),
        key=lambda d: -(min(d[0], 4 - d[0]) + min(d[1], 4 - d[1])),
    )
)


def on_device(history, free_rows, memory_start, now):
    vmem = pltpu.VMEM
    dma = pltpu.SemaphoreType.DMA
    result = pl.pallas_call(
        kernel,
        out_shape=jax.ShapeDtypeStruct((2, 2, 256, 128), BF16),
        in_specs=[
            pl.BlockSpec(memory_space=pl.ANY),
            pl.BlockSpec(memory_space=pl.ANY),
            pl.BlockSpec(memory_space=pltpu.SMEM),
            pl.BlockSpec(memory_space=pltpu.SMEM),
        ],
        out_specs=pl.BlockSpec(memory_space=pltpu.VMEM),
        scratch_shapes=[
            vmem((2, 4, 256, 128), BF16),
            vmem((4, 2, 256, 128), F32),
            vmem((4, 2, 512, 512), BF16),
            vmem((2, 2, 256, 128), BF16),
            vmem((2, 2, 64, 128), F32),
            vmem((2, 2, 64, 128), BF16),
            vmem((64, 128), BF16),
            vmem((64, 128), BF16),
            vmem((ITERS, 64, 128), BF16),
            vmem((ITERS, 4, 4, 64, 128), BF16),
            vmem((ITERS, 4, 64, 128), BF16),
            vmem((ITERS, 4, 64, 128), BF16),
            vmem((64, 128), BF16),
            vmem((4, 2, 2, 64, 128), BF16),
            vmem((2, 2, 256, 128), F32),
            dma((2,)),
            dma((12,)), dma((12,)),
            dma((16,)), dma((16,)),
            dma((5,)), dma((2,)),
            dma((ITERS, 16)), dma((ITERS, 4, 4)),
            dma((ITERS, 4)), dma((ITERS, 4)),
            dma((4,)), dma((2, 2)),
            dma((12,)), dma((4, 2, 2)),
        ],
        compiler_params=pltpu.CompilerParams(
            collective_id=0, has_side_effects=True, vmem_limit_bytes=48 * 1024 * 1024
        ),
        name="fixed_point",
    )(history.reshape(2, 4, 256, 128), free_rows.reshape(2, 2, 256, 128), memory_start, now)
    return result.reshape(free_rows.shape)


def solution(mesh):
    return jax.shard_map(
        on_device,
        mesh=mesh,
        in_specs=(P(None, "mem", None, "tt", None), P(None, None, None, "tt", None), P(), P()),
        out_specs=P(None, None, None, "tt", None),
        check_vma=False,
    )
```

```python
import functools

import jax
import jax.numpy as jnp
from jax import lax
from jax.experimental import pallas as pl
from jax.experimental.pallas import tpu as pltpu
from jax.sharding import PartitionSpec as P

ITERS = 3
COUPLING = 0.5
MESH = pl.DeviceIdType.MESH
BF16 = jnp.bfloat16
F32 = jnp.float32
CHUNKS = 2
VMEM_KIB = 54784
ROWS = 32 // CHUNKS


def device(x, y, zh, zl, c):
    return (y * 4 + zh, x * 8 + zl * 2 + c)


def kernel(
    hist, free, start, now, out,
    start_s, now_s, hraw, htmp, h_all, fraw, ftmp, fpc, fa, fb, gsend, grecv, rsend, rrecv, xfin, pieces, otmp,
    lsem, hy_s, hy_r, hs_s, hs_r, f_s, f_r, g_s, g_r, r_s, r_r, az_s, az_r, ay_s, ay_r, known,
):
    mem, tt = lax.axis_index("mem"), lax.axis_index("tt")
    y, zh = mem // 4, mem % 4
    x, zl, c = tt // 8, (tt // 2) % 4, tt % 2
    sib = device(x, y, zh, zl, 1 - c)

    def remote(src, dst, ssem, rsem, dev):
        return pltpu.make_async_remote_copy(
            src_ref=src, dst_ref=dst, send_sem=ssem, recv_sem=rsem, device_id=dev, device_id_type=MESH
        )

    load_h = pltpu.make_async_copy(hist, hraw, lsem.at[0])
    load_f = pltpu.make_async_copy(free, fraw, lsem.at[1])
    load_s = pltpu.make_async_copy(start, start_s, lsem.at[2])
    load_n = pltpu.make_async_copy(now, now_s, lsem.at[3])
    load_h.start()
    load_f.start()
    load_s.start()
    load_n.start()

    def z_dev(d):
        z = (zh * 4 + zl + d + 16) % 16
        return device(x, y, z // 4, z % 4, c)

    def x_dev(d):
        return device((x + d) % 4, y, zh, zl, c)

    up, down, far = (y + 1) % 4, (y + 3) % 4, (y + 2) % 4
    up_dev, down_dev = device(x, up, zh, zl, c), device(x, down, zh, zl, c)

    def tell(sem, devs):
        for dev in devs:
            pl.semaphore_signal(sem, inc=1, device_id=dev, device_id_type=MESH)

    barrier = pltpu.get_barrier_semaphore()
    tell(barrier, (up_dev, down_dev, sib, x_dev(1), x_dev(3), z_dev(1), z_dev(-1)))

    load_f.wait()
    for part in range(2):
        for r in range(2):
            rows = pl.ds(pl.multiple_of(y * 64, 64), 64)
            ftmp[part, r] = fraw[part, r, rows, :].astype(F32)
    for part in range(2):
        for r in range(2):
            for t in range(2):
                for ch in range(CHUNKS):
                    at = pl.ds(ch * 2 * ROWS + t, ROWS, stride=2)
                    fpc[t, r, ch, part * ROWS : part * ROWS + ROWS, :] = ftmp[part, r, at, :].astype(BF16)

    load_h.wait()
    for sl in range(4):
        for part in range(2):
            htmp[sl, part] = hraw[part, sl].astype(F32)
        for part in range(2):
            for t in range(2):
                col = (t * 2 + part) * 128
                h_all[y, c, sl * 128 : sl * 128 + 128, col : col + 128] = htmp[
                    sl, part, pl.ds(t, 128, stride=2), :
                ].astype(BF16)

    pl.semaphore_wait(barrier, 7)
    tell(known.at[0], (x_dev(1), x_dev(3), z_dev(1), z_dev(-1)))
    sends = []

    def slab(b, core, sl):
        return h_all.at[b, core, pl.ds(sl * 128, 128), :]

    def hy(b, sl, k, dev):
        cp = remote(slab(b, c, sl), slab(b, c, sl), hy_s.at[k], hy_r.at[k], dev)
        cp.start()
        sends.append(cp)

    def hs(b, sl, k):
        cp = remote(slab(b, c, sl), slab(b, c, sl), hs_s.at[k], hs_r.at[k], sib)
        cp.start()
        sends.append(cp)

    def hy_wait(b, sl, k):
        remote(slab(b, c, sl), slab(b, c, sl), hy_s.at[k], hy_r.at[k], up_dev).wait_recv()

    for k in range(2):
        hy(y, k, k, up_dev)
        hy(y, k + 2, 4 + k, down_dev)
    for k in range(4):
        hs(y, k, k)

    pl.semaphore_wait(known.at[0], 4)
    tell(known.at[1], (z_dev(2), z_dev(-2)))

    @pl.when(c == zh // 2)
    def _():
        fb[...] = fpc[zh % 2, c]
        remote(fpc.at[zh % 2, 1 - c], fb, f_s.at[4], f_r.at[1], sib).start()

    load_s.wait()
    load_n.wait()
    pl.semaphore_wait(known.at[1], 2)
    tell(known.at[2], (z_dev(4), z_dev(-4)))
    tell(known.at[3], (x_dev(1), x_dev(3), x_dev(2)))

    for t in range(2):
        for r in range(2):
            to = 2 * c + t
            mine = (zl == to) & (c == r)

            @pl.when((zl == zh) & mine)
            def _():
                fa[...] = fpc[t, r]

            @pl.when((zl == zh) & jnp.logical_not(mine))
            def _():
                remote(fpc.at[t, r], fa, f_s.at[t * 2 + r], f_r.at[0], device(x, y, zh, to, r)).start()

    for k in range(2):
        hy(y, k + 2, 2 + k, up_dev)
        hy(y, k, 6 + k, down_dev)
    pl.semaphore_wait(known.at[3], 3)
    for k in range(2):
        hy_wait(down, k, k)
        hy(down, k, 8 + k, up_dev)
        hs(down, k, 4 + k)
        hy_wait(up, k + 2, 4 + k)
        hy(up, k + 2, 10 + k, down_dev)
        hs(up, k + 2, 8 + k)

    @pl.when(jnp.logical_not((zl == zh) & (c == zl // 2)))
    def _():
        remote(fpc.at[0, 0], fa, f_s.at[0], f_r.at[0], sib).wait_recv()

    s_time = 16 * x + 4 * zh + zl
    live = jnp.where((start_s[c] <= s_time) & (s_time < now_s[0] + c), 1.0, 0.0).astype(F32)

    def gather(n, ch, value):
        re, im = value[:ROWS].astype(F32), value[ROWS:].astype(F32)
        mod = re * re + im * im
        gsend[n, ch, :ROWS, :] = (-(re * mod) * live).astype(BF16)
        gsend[n, ch, ROWS:, :] = (-(im * mod) * live).astype(BF16)
        for dx, dz in G_ORDER:
            dev = device((x + dx) % 4, y, zh, (zl + dz) % 4, c)
            cp = remote(gsend.at[n, ch], grecv.at[n, ch, x, zl], g_s.at[n, ch, dx * 4 + dz], g_r.at[n, ch, x, zl], dev)
            cp.start()
            sends.append(cp)
        grecv[n, ch, x, zl] = gsend[n, ch]

    def g_wait(n, ch, dx):
        for dz in range(4):
            if dx or dz:
                xs, zs = (x + dx) % 4, (zl + dz) % 4
                b = grecv.at[n, ch, xs, zs]
                remote(b, b, g_s.at[n, ch, 0], g_r.at[n, ch, xs, zs], sib).wait_recv()

    def product(n, ch, b, core):
        left = jnp.concatenate([grecv[n, ch, b, sl] for sl in range(4)], axis=1)
        return jnp.dot(left, h_all[b, core], preferred_element_type=F32)

    def r_blocks(n, ch, acc):
        for t in range(4):
            p = acc[t // 2][:, (t % 2) * 256 : (t % 2) * 256 + 256]
            rsend[n, ch, t, :ROWS, :] = (p[:ROWS, :128] - p[ROWS:, 128:]).astype(BF16)
            rsend[n, ch, t, ROWS:, :] = (p[:ROWS, 128:] + p[ROWS:, :128]).astype(BF16)

    def multiply(n, ch):
        acc = [None, None]
        for d in (0, 1, 3, 2):
            g_wait(n, ch, d)
            for core in range(2):
                prod = product(n, ch, (x + d) % 4, core)
                acc[core] = prod if acc[core] is None else acc[core] + prod
        r_blocks(n, ch, acc)

    def r_here(last, t):
        return (zh == t) if last else (zh == zl) & (zl == t)

    def r_send(n, ch, last):
        for t in range(4):
            dev = device(x, y, t, zl, c) if last else device(x, y, zl, t, c)

            @pl.when(r_here(last, t))
            def _():
                rrecv[n, ch, zh] = rsend[n, ch, t]

            @pl.when(jnp.logical_not(r_here(last, t)))
            def _():
                remote(rsend.at[n, ch, t], rrecv.at[n, ch, zh], r_s.at[n, ch, t], r_r.at[n, ch, zh], dev).start()

    def r_sum(n, ch, last, base):
        for src in range(4):
            here = (zh == src) if last else (zh == zl) & (zh == src)

            @pl.when(jnp.logical_not(here))
            def _():
                b = rrecv.at[n, ch, src]
                remote(b, b, r_s.at[n, ch, src], r_r.at[n, ch, src], sib).wait_recv()

        total = sum(rrecv[n, ch, src].astype(F32) for src in range(4))
        return (base[ch].astype(F32) + COUPLING * total).astype(BF16)

    def flush():
        for cp in sends:
            cp.wait_send()
        sends.clear()

    for ch in range(CHUNKS):
        gather(0, ch, fa[ch])

    for k in range(2):
        hy_wait(down, k + 2, 2 + k)
        hs(down, k + 2, 6 + k)
        hy_wait(up, k, 6 + k)
        hs(up, k, 10 + k)
    pl.semaphore_wait(known.at[2], 2)

    def hs_wait(b, slabs):
        for sl, k in slabs:
            remote(slab(b, 1 - c, sl), slab(b, 1 - c, sl), hs_s.at[k], hs_r.at[k], sib).wait_recv()

    for ch in range(CHUNKS):
        for d in range(4):
            g_wait(0, ch, d)
    hs_wait(y, ((0, 0), (1, 1), (2, 2), (3, 3)))
    hs_wait(down, ((0, 4), (1, 5), (2, 6), (3, 7)))
    hs_wait(up, ((2, 8), (3, 9), (0, 10), (1, 11)))
    own = [sum(product(0, ch, b, c) for b in (y, down, up)) for ch in range(CHUNKS)]
    other = [sum(product(0, ch, b, 1 - c) for b in (y, down, up)) for ch in range(CHUNKS)]
    for k in range(2):
        hy_wait(far, k, 8 + k)
        hs(far, k, 12 + k)
        hy_wait(far, k + 2, 10 + k)
        hs(far, k + 2, 14 + k)
    own = [own[ch] + product(0, ch, far, c) for ch in range(CHUNKS)]
    hs_wait(far, ((0, 12), (1, 13), (2, 14), (3, 15)))

    for n in range(ITERS):
        last = n == ITERS - 1
        for ch in range(CHUNKS):
            if n == 0:
                rest = other[ch] + product(0, ch, far, 1 - c)
                r_blocks(0, ch, [jnp.where(c == 0, own[ch], rest), jnp.where(c == 0, rest, own[ch])])
            else:
                multiply(n, ch)
            r_send(n, ch, last)
        flush()
        if not last:
            for ch in range(CHUNKS):
                gather(n + 1, ch, r_sum(n, ch, last, fa))

    @pl.when(c != zh // 2)
    def _():
        remote(fpc.at[0, 0], fb, f_s.at[4], f_r.at[1], sib).wait_recv()

    core = zh // 2
    for ch in range(CHUNKS):
        xfin[ch] = r_sum(ITERS - 1, ch, True, fb)
        for d in (2, 1, 3, 0):
            dev = device(x, y, (zh + d) % 4, zl, core)

            def go(d=d, dev=dev):
                remote(xfin.at[ch], pieces.at[y, zh % 2, c, ch], az_s.at[ch, d], az_r.at[zh % 2, c, ch], dev).start()

            if d:
                go()
            else:
                @pl.when(core != c)
                def _():
                    go()

                @pl.when(core == c)
                def _():
                    pieces[y, zh % 2, c, ch] = xfin[ch]

    near = jnp.where((zh == 2 * c) | (zh == (2 * c + 3) % 4), 0, 1)
    for order in range(2):
        t = near if order == 0 else 1 - near
        for ch in range(CHUNKS):
            for r in range(2):
                src = pieces.at[y, t, r, ch]

                @pl.when(jnp.logical_not((zh == 2 * c + t) & (c == r)))
                def _():
                    remote(src, src, az_s.at[0, 0], az_r.at[t, r, ch], sib).wait_recv()

                for dy in (2, 1, 3):
                    k = (order * 2 + r) * CHUNKS + ch
                    dev = device(x, (y + dy) % 4, zh, zl, c)
                    cp = remote(src, src, ay_s.at[dy - 1, k], ay_r.at[y, t, r, ch], dev)
                    cp.start()
                    sends.append(cp)

    def assemble(b):
        for t in range(2):
            for r in range(2):
                for part in range(2):
                    for ch in range(CHUNKS):
                        at = pl.ds(pl.multiple_of(b * 64, 64) + ch * 2 * ROWS + t, ROWS, stride=2)
                        otmp[part, r, at, :] = pieces[b, t, r, ch, part * ROWS : part * ROWS + ROWS, :].astype(F32)
        for r in range(2):
            for part in range(2):
                rows = pl.ds(pl.multiple_of(b * 64, 64), 64)
                out[part, r, rows, :] = otmp[part, r, rows, :].astype(BF16)

    assemble(y)
    for dy in (1, 3, 2):
        b = (y + dy) % 4
        for t in range(2):
            for r in range(2):
                for ch in range(CHUNKS):
                    p = pieces.at[b, t, r, ch]
                    remote(p, p, ay_s.at[0, 0], ay_r.at[b, t, r, ch], sib).wait_recv()
        assemble(b)

    for t in range(2):
        for r in range(2):
            @pl.when((zl == zh) & jnp.logical_not((zl == 2 * c + t) & (c == r)))
            def _():
                remote(fpc.at[t, r], fa, f_s.at[t * 2 + r], f_r.at[0], sib).wait_send()

    @pl.when(c == zh // 2)
    def _():
        remote(fpc.at[0, 0], fb, f_s.at[4], f_r.at[1], sib).wait_send()

    for n in range(ITERS):
        for ch in range(CHUNKS):
            for t in range(4):
                @pl.when(jnp.logical_not(r_here(n == ITERS - 1, t)))
                def _():
                    b = rsend.at[n, ch, t]
                    remote(b, b, r_s.at[n, ch, t], r_r.at[n, ch, t], sib).wait_send()
    for ch in range(CHUNKS):
        for d in range(4):
            def done(d=d):
                remote(xfin.at[ch], xfin.at[ch], az_s.at[ch, d], az_r.at[0, 0, ch], sib).wait_send()

            if d:
                done()
            else:
                pl.when(core != c)(done)
    flush()


G_ORDER = tuple(
    sorted(
        ((dx, dz) for dx in range(4) for dz in range(4) if dx or dz),
        key=lambda d: -(min(d[0], 4 - d[0]) + min(d[1], 4 - d[1])),
    )
)


def on_device(history, free_rows, memory_start, now):
    vmem = pltpu.VMEM
    dma = pltpu.SemaphoreType.DMA
    block = (CHUNKS, 2 * ROWS, 128)
    result = pl.pallas_call(
        kernel,
        out_shape=jax.ShapeDtypeStruct((2, 2, 256, 128), BF16),
        in_specs=[pl.BlockSpec(memory_space=pltpu.HBM)] * 4,
        out_specs=pl.BlockSpec(memory_space=pltpu.VMEM),
        scratch_shapes=[
            pltpu.SMEM((2,), jnp.int32),
            pltpu.SMEM((1,), jnp.int32),
            vmem((2, 4, 256, 128), BF16),
            vmem((4, 2, 256, 128), F32),
            vmem((4, 2, 512, 512), BF16),
            vmem((2, 2, 256, 128), BF16),
            vmem((2, 2, 64, 128), F32),
            vmem((2, 2, *block), BF16),
            vmem(block, BF16),
            vmem(block, BF16),
            vmem((ITERS, *block), BF16),
            vmem((ITERS, CHUNKS, 4, 4, *block[1:]), BF16),
            vmem((ITERS, CHUNKS, 4, *block[1:]), BF16),
            vmem((ITERS, CHUNKS, 4, *block[1:]), BF16),
            vmem(block, BF16),
            vmem((4, 2, 2, *block), BF16),
            vmem((2, 2, 256, 128), F32),
            dma((4,)),
            dma((12,)), dma((12,)),
            dma((16,)), dma((16,)),
            dma((5,)), dma((2,)),
            dma((ITERS, CHUNKS, 16)), dma((ITERS, CHUNKS, 4, 4)),
            dma((ITERS, CHUNKS, 4)), dma((ITERS, CHUNKS, 4)),
            dma((CHUNKS, 4)), dma((2, 2, CHUNKS)),
            dma((3, 4 * CHUNKS)), dma((4, 2, 2, CHUNKS)),
            pltpu.SemaphoreType.REGULAR((4,)),
        ],
        compiler_params=pltpu.CompilerParams(
            collective_id=0, has_side_effects=True, vmem_limit_bytes=VMEM_KIB * 1024
        ),
        name="fixed_point",
    )(history.reshape(2, 4, 256, 128), free_rows.reshape(2, 2, 256, 128), memory_start, now)
    return result.reshape(free_rows.shape)


def solution(mesh):
    return jax.shard_map(
        on_device,
        mesh=mesh,
        in_specs=(P(None, "mem", None, "tt", None), P(None, None, None, "tt", None), P(), P()),
        out_specs=P(None, None, None, "tt", None),
        check_vma=False,
    )
```

```python
import functools

import jax
import jax.numpy as jnp
from jax import lax
from jax.experimental import pallas as pl
from jax.experimental.pallas import tpu as pltpu
from jax.sharding import PartitionSpec as P

ITERS = 3
COUPLING = 0.5
MESH = pl.DeviceIdType.MESH
BF16 = jnp.bfloat16
F32 = jnp.float32
CHUNKS = 2
VMEM_KIB = 54784
ROWS = 32 // CHUNKS


def device(x, y, zh, zl, c):
    return (y * 4 + zh, x * 8 + zl * 2 + c)


def kernel(
    hist, free, start, now, out,
    start_s, now_s, hraw, htmp, h_all, fraw, ftmp, fpc, fa, fb, gsend, grecv, gsib, rsend, rrecv, xfin, pieces, otmp,
    lsem, hy_s, hy_r, hs_s, hs_r, f_s, f_r, g_s, g_r, gs_s, gs_r, r_s, r_r, az_s, az_r, ay_s, ay_r, known,
):
    mem, tt = lax.axis_index("mem"), lax.axis_index("tt")
    y, zh = mem // 4, mem % 4
    x, zl, c = tt // 8, (tt // 2) % 4, tt % 2
    sib = device(x, y, zh, zl, 1 - c)

    def remote(src, dst, ssem, rsem, dev):
        return pltpu.make_async_remote_copy(
            src_ref=src, dst_ref=dst, send_sem=ssem, recv_sem=rsem, device_id=dev, device_id_type=MESH
        )

    load_h = pltpu.make_async_copy(hist, hraw, lsem.at[0])
    load_f = pltpu.make_async_copy(free, fraw, lsem.at[1])
    load_s = pltpu.make_async_copy(start, start_s, lsem.at[2])
    load_n = pltpu.make_async_copy(now, now_s, lsem.at[3])
    load_h.start()
    load_f.start()
    load_s.start()
    load_n.start()

    def z_dev(d):
        z = (zh * 4 + zl + d + 16) % 16
        return device(x, y, z // 4, z % 4, c)

    def x_dev(d):
        return device((x + d) % 4, y, zh, zl, c)

    up, down, far = (y + 1) % 4, (y + 3) % 4, (y + 2) % 4
    up_dev, down_dev = device(x, up, zh, zl, c), device(x, down, zh, zl, c)

    def tell(sem, devs):
        for dev in devs:
            pl.semaphore_signal(sem, inc=1, device_id=dev, device_id_type=MESH)

    barrier = pltpu.get_barrier_semaphore()
    tell(barrier, (up_dev, down_dev, sib, x_dev(1), x_dev(3), z_dev(1), z_dev(-1)))

    load_f.wait()
    for part in range(2):
        for r in range(2):
            rows = pl.ds(pl.multiple_of(y * 64, 64), 64)
            ftmp[part, r] = fraw[part, r, rows, :].astype(F32)
    for part in range(2):
        for r in range(2):
            for t in range(2):
                for ch in range(CHUNKS):
                    at = pl.ds(ch * 2 * ROWS + t, ROWS, stride=2)
                    fpc[t, r, ch, part * ROWS : part * ROWS + ROWS, :] = ftmp[part, r, at, :].astype(BF16)

    load_h.wait()
    for sl in range(4):
        for part in range(2):
            htmp[sl, part] = hraw[part, sl].astype(F32)
        for part in range(2):
            for t in range(2):
                col = (t * 2 + part) * 128
                h_all[y, c, sl * 128 : sl * 128 + 128, col : col + 128] = htmp[
                    sl, part, pl.ds(t, 128, stride=2), :
                ].astype(BF16)

    pl.semaphore_wait(barrier, 7)
    tell(known.at[0], (x_dev(1), x_dev(3), z_dev(1), z_dev(-1)))
    sends = []

    def slab(b, core, sl):
        return h_all.at[b, core, pl.ds(sl * 128, 128), :]

    def hy(b, sl, k, dev):
        cp = remote(slab(b, c, sl), slab(b, c, sl), hy_s.at[k], hy_r.at[k], dev)
        cp.start()
        sends.append(cp)

    def hs(b, sl, k):
        cp = remote(slab(b, c, sl), slab(b, c, sl), hs_s.at[k], hs_r.at[k], sib)
        cp.start()
        sends.append(cp)

    def hy_wait(b, sl, k):
        remote(slab(b, c, sl), slab(b, c, sl), hy_s.at[k], hy_r.at[k], up_dev).wait_recv()

    for k in range(2):
        hy(y, k, k, up_dev)
        hy(y, k + 2, 4 + k, down_dev)
    for k in range(4):
        hs(y, k, k)

    pl.semaphore_wait(known.at[0], 4)
    tell(known.at[1], (z_dev(2), z_dev(-2)))

    @pl.when(c == zh // 2)
    def _():
        fb[...] = fpc[zh % 2, c]
        remote(fpc.at[zh % 2, 1 - c], fb, f_s.at[4], f_r.at[1], sib).start()

    load_s.wait()
    load_n.wait()
    pl.semaphore_wait(known.at[1], 2)
    tell(known.at[2], (z_dev(4), z_dev(-4)))
    tell(known.at[3], (x_dev(1), x_dev(3), x_dev(2)))

    for t in range(2):
        for r in range(2):
            to = 2 * c + t
            mine = (zl == to) & (c == r)

            @pl.when((zl == zh) & mine)
            def _():
                fa[...] = fpc[t, r]

            @pl.when((zl == zh) & jnp.logical_not(mine))
            def _():
                remote(fpc.at[t, r], fa, f_s.at[t * 2 + r], f_r.at[0], device(x, y, zh, to, r)).start()

    for k in range(2):
        hy(y, k + 2, 2 + k, up_dev)
        hy(y, k, 6 + k, down_dev)
    pl.semaphore_wait(known.at[3], 3)
    for k in range(2):
        hy_wait(down, k, k)
        hy(down, k, 8 + k, up_dev)
        hs(down, k, 4 + k)
        hy_wait(up, k + 2, 4 + k)
        hy(up, k + 2, 10 + k, down_dev)
        hs(up, k + 2, 8 + k)

    @pl.when(jnp.logical_not((zl == zh) & (c == zl // 2)))
    def _():
        remote(fpc.at[0, 0], fa, f_s.at[0], f_r.at[0], sib).wait_recv()

    s_time = 16 * x + 4 * zh + zl
    live = jnp.where((start_s[c] <= s_time) & (s_time < now_s[0] + c), 1.0, 0.0).astype(F32)

    def gather(n, ch, value):
        re, im = value[:ROWS].astype(F32), value[ROWS:].astype(F32)
        mod = re * re + im * im
        gsend[n, ch, :ROWS, :] = (-(re * mod) * live).astype(BF16)
        gsend[n, ch, ROWS:, :] = (-(im * mod) * live).astype(BF16)
        for dx, dz in G_ORDER:
            dev = device((x + dx) % 4, y, zh, (zl + dz) % 4, c)
            cp = remote(gsend.at[n, ch], grecv.at[n, ch, x, zl], g_s.at[n, ch, dx * 4 + dz], g_r.at[n, ch, x, zl], dev)
            cp.start()
            sends.append(cp)
        grecv[n, ch, x, zl] = gsend[n, ch]

    def g_wait(n, ch, dx):
        for dz in range(4):
            if dx or dz:
                xs, zs = (x + dx) % 4, (zl + dz) % 4
                b = grecv.at[n, ch, xs, zs]
                remote(b, b, g_s.at[n, ch, 0], g_r.at[n, ch, xs, zs], sib).wait_recv()

    def product(n, ch, b, core):
        left = jnp.concatenate([grecv[n, ch, b, sl] for sl in range(4)], axis=1)
        return jnp.dot(left, h_all[b, core], preferred_element_type=F32)

    def r_block(n, ch, t, p):
        rsend[n, ch, t, :ROWS, :] = (p[:ROWS, :128] - p[ROWS:, 128:]).astype(BF16)
        rsend[n, ch, t, ROWS:, :] = (p[:ROWS, 128:] + p[ROWS:, :128]).astype(BF16)

    def multiply(n, ch):
        acc = [None, None]
        for d in (0, 1, 3, 2):
            g_wait(n, ch, d)
            for core in range(2):
                prod = product(n, ch, (x + d) % 4, core)
                acc[core] = prod if acc[core] is None else acc[core] + prod
        for t in range(4):
            r_block(n, ch, t, acc[t // 2][:, (t % 2) * 256 : (t % 2) * 256 + 256])

    def r_dest(n, t):
        if n == ITERS - 1 and n > 0:
            return device(x, y, t, zl, c)
        if n > 0:
            return device(x, y, zl, t, c)
        return device(x, y, zl, 2 * c + t % 2, c if t < 2 else 1 - c)

    def r_here(n, t):
        if n == ITERS - 1 and n > 0:
            return zh == t
        if n > 0:
            return (zh == zl) & (zl == t)
        return (zh == zl) & (zl == 2 * c + t % 2) if t < 2 else False

    def r_send(n, ch):
        for t in range(4):
            if r_here(n, t) is not False:

                @pl.when(r_here(n, t))
                def _():
                    rrecv[n, ch, zh] = rsend[n, ch, t]

            @pl.when(jnp.logical_not(r_here(n, t)))
            def _():
                remote(rsend.at[n, ch, t], rrecv.at[n, ch, zh], r_s.at[n, ch, t], r_r.at[n, ch, zh], r_dest(n, t)).start()

    def r_sum(n, ch, base):
        for src in range(4):
            if n == ITERS - 1 and n > 0:
                here = zh == src
            elif n > 0:
                here = (zh == zl) & (zh == src)
            else:
                here = (zh == zl) & (zh == src) & (c == zl // 2)

            @pl.when(jnp.logical_not(here))
            def _():
                b = rrecv.at[n, ch, src]
                remote(b, b, r_s.at[n, ch, src], r_r.at[n, ch, src], sib).wait_recv()

        total = sum(rrecv[n, ch, src].astype(F32) for src in range(4))
        return (base[ch].astype(F32) + COUPLING * total).astype(BF16)

    def flush():
        for cp in sends:
            cp.wait_send()
        sends.clear()

    for ch in range(CHUNKS):
        gather(0, ch, fa[ch])

    for k in range(2):
        hy_wait(down, k + 2, 2 + k)
        hs(down, k + 2, 6 + k)
        hy_wait(up, k, 6 + k)
        hs(up, k, 10 + k)
    pl.semaphore_wait(known.at[2], 2)
    tell(known.at[4], (sib,))

    for ch in range(CHUNKS):
        for d in range(4):
            g_wait(0, ch, d)
        cp = remote(grecv.at[0, ch], gsib.at[ch], gs_s.at[ch], gs_r.at[ch], sib)
        cp.start()
        sends.append(cp)
    for ch in range(CHUNKS):
        remote(gsib.at[ch], gsib.at[ch], gs_s.at[ch], gs_r.at[ch], sib).wait_recv()

    def first(b):
        left = [[jnp.concatenate([g[b, sl] for sl in range(4)], axis=1) for g in (grecv.at[0, ch], gsib.at[ch])]
                for ch in range(CHUNKS)]
        return jnp.dot(jnp.concatenate(sum(left, []), axis=0), h_all[b, c], preferred_element_type=F32)

    acc = first(y) + first(down) + first(up)
    for k in range(2):
        hy_wait(far, k, 8 + k)
        hy_wait(far, k + 2, 10 + k)
    acc = acc + first(far)
    pl.semaphore_wait(known.at[4], 1)
    for ch in range(CHUNKS):
        for t in range(4):
            at = (ch * 2 + t // 2) * 2 * ROWS
            r_block(0, ch, t, acc[at : at + 2 * ROWS, (t % 2) * 256 : (t % 2) * 256 + 256])
        r_send(0, ch)
    for k in range(2):
        hs(far, k, 12 + k)
        hs(far, k + 2, 14 + k)
    for b, slabs in (
        (y, ((0, 0), (1, 1), (2, 2), (3, 3))),
        (down, ((0, 4), (1, 5), (2, 6), (3, 7))),
        (up, ((2, 8), (3, 9), (0, 10), (1, 11))),
        (far, ((0, 12), (1, 13), (2, 14), (3, 15))),
    ):
        for sl, k in slabs:
            remote(slab(b, 1 - c, sl), slab(b, 1 - c, sl), hs_s.at[k], hs_r.at[k], sib).wait_recv()

    for n in range(1, ITERS):
        flush()
        for ch in range(CHUNKS):
            gather(n, ch, r_sum(n - 1, ch, fa))
        for ch in range(CHUNKS):
            multiply(n, ch)
            r_send(n, ch)
    flush()

    @pl.when(c != zh // 2)
    def _():
        remote(fpc.at[0, 0], fb, f_s.at[4], f_r.at[1], sib).wait_recv()

    core = zh // 2
    for ch in range(CHUNKS):
        xfin[ch] = r_sum(ITERS - 1, ch, fb)
        for d in (2, 1, 3, 0):
            dev = device(x, y, (zh + d) % 4, zl, core)

            def go(d=d, dev=dev):
                remote(xfin.at[ch], pieces.at[y, zh % 2, c, ch], az_s.at[ch, d], az_r.at[zh % 2, c, ch], dev).start()

            if d:
                go()
            else:
                @pl.when(core != c)
                def _():
                    go()

                @pl.when(core == c)
                def _():
                    pieces[y, zh % 2, c, ch] = xfin[ch]

    near = jnp.where((zh == 2 * c) | (zh == (2 * c + 3) % 4), 0, 1)
    for order in range(2):
        t = near if order == 0 else 1 - near
        for ch in range(CHUNKS):
            for r in range(2):
                src = pieces.at[y, t, r, ch]

                @pl.when(jnp.logical_not((zh == 2 * c + t) & (c == r)))
                def _():
                    remote(src, src, az_s.at[0, 0], az_r.at[t, r, ch], sib).wait_recv()

                for dy in (2, 1, 3):
                    k = (order * 2 + r) * CHUNKS + ch
                    dev = device(x, (y + dy) % 4, zh, zl, c)
                    cp = remote(src, src, ay_s.at[dy - 1, k], ay_r.at[y, t, r, ch], dev)
                    cp.start()
                    sends.append(cp)

    def assemble(b):
        for t in range(2):
            for r in range(2):
                for part in range(2):
                    for ch in range(CHUNKS):
                        at = pl.ds(pl.multiple_of(b * 64, 64) + ch * 2 * ROWS + t, ROWS, stride=2)
                        otmp[part, r, at, :] = pieces[b, t, r, ch, part * ROWS : part * ROWS + ROWS, :].astype(F32)
        for r in range(2):
            for part in range(2):
                rows = pl.ds(pl.multiple_of(b * 64, 64), 64)
                out[part, r, rows, :] = otmp[part, r, rows, :].astype(BF16)

    assemble(y)
    for dy in (1, 3, 2):
        b = (y + dy) % 4
        for t in range(2):
            for r in range(2):
                for ch in range(CHUNKS):
                    p = pieces.at[b, t, r, ch]
                    remote(p, p, ay_s.at[0, 0], ay_r.at[b, t, r, ch], sib).wait_recv()
        assemble(b)

    for t in range(2):
        for r in range(2):
            @pl.when((zl == zh) & jnp.logical_not((zl == 2 * c + t) & (c == r)))
            def _():
                remote(fpc.at[t, r], fa, f_s.at[t * 2 + r], f_r.at[0], sib).wait_send()

    @pl.when(c == zh // 2)
    def _():
        remote(fpc.at[0, 0], fb, f_s.at[4], f_r.at[1], sib).wait_send()

    for n in range(ITERS):
        for ch in range(CHUNKS):
            for t in range(4):
                @pl.when(jnp.logical_not(r_here(n, t)))
                def _():
                    b = rsend.at[n, ch, t]
                    remote(b, b, r_s.at[n, ch, t], r_r.at[n, ch, t], sib).wait_send()
    for ch in range(CHUNKS):
        for d in range(4):
            def done(d=d):
                remote(xfin.at[ch], xfin.at[ch], az_s.at[ch, d], az_r.at[0, 0, ch], sib).wait_send()

            if d:
                done()
            else:
                pl.when(core != c)(done)
    flush()


G_ORDER = tuple(
    sorted(
        ((dx, dz) for dx in range(4) for dz in range(4) if dx or dz),
        key=lambda d: -(min(d[0], 4 - d[0]) + min(d[1], 4 - d[1])),
    )
)


def on_device(history, free_rows, memory_start, now):
    vmem = pltpu.VMEM
    dma = pltpu.SemaphoreType.DMA
    block = (CHUNKS, 2 * ROWS, 128)
    result = pl.pallas_call(
        kernel,
        out_shape=jax.ShapeDtypeStruct((2, 2, 256, 128), BF16),
        in_specs=[pl.BlockSpec(memory_space=pltpu.HBM)] * 4,
        out_specs=pl.BlockSpec(memory_space=pltpu.VMEM),
        scratch_shapes=[
            pltpu.SMEM((2,), jnp.int32),
            pltpu.SMEM((1,), jnp.int32),
            vmem((2, 4, 256, 128), BF16),
            vmem((4, 2, 256, 128), F32),
            vmem((4, 2, 512, 512), BF16),
            vmem((2, 2, 256, 128), BF16),
            vmem((2, 2, 64, 128), F32),
            vmem((2, 2, *block), BF16),
            vmem(block, BF16),
            vmem(block, BF16),
            vmem((ITERS, *block), BF16),
            vmem((ITERS, CHUNKS, 4, 4, *block[1:]), BF16),
            vmem((CHUNKS, 4, 4, *block[1:]), BF16),
            vmem((ITERS, CHUNKS, 4, *block[1:]), BF16),
            vmem((ITERS, CHUNKS, 4, *block[1:]), BF16),
            vmem(block, BF16),
            vmem((4, 2, 2, *block), BF16),
            vmem((2, 2, 256, 128), F32),
            dma((4,)),
            dma((12,)), dma((12,)),
            dma((16,)), dma((16,)),
            dma((5,)), dma((2,)),
            dma((ITERS, CHUNKS, 16)), dma((ITERS, CHUNKS, 4, 4)),
            dma((CHUNKS,)), dma((CHUNKS,)),
            dma((ITERS, CHUNKS, 4)), dma((ITERS, CHUNKS, 4)),
            dma((CHUNKS, 4)), dma((2, 2, CHUNKS)),
            dma((3, 4 * CHUNKS)), dma((4, 2, 2, CHUNKS)),
            pltpu.SemaphoreType.REGULAR((5,)),
        ],
        compiler_params=pltpu.CompilerParams(
            collective_id=0, has_side_effects=True, vmem_limit_bytes=VMEM_KIB * 1024
        ),
        name="fixed_point",
    )(history.reshape(2, 4, 256, 128), free_rows.reshape(2, 2, 256, 128), memory_start, now)
    return result.reshape(free_rows.shape)


def solution(mesh):
    return jax.shard_map(
        on_device,
        mesh=mesh,
        in_specs=(P(None, "mem", None, "tt", None), P(None, None, None, "tt", None), P(), P()),
        out_specs=P(None, None, None, "tt", None),
        check_vma=False,
    )
```

```python
import functools

import jax
import jax.numpy as jnp
from jax import lax
from jax.experimental import pallas as pl
from jax.experimental.pallas import tpu as pltpu
from jax.sharding import PartitionSpec as P

ITERS = 3
COUPLING = 0.5
MESH = pl.DeviceIdType.MESH
BF16 = jnp.bfloat16
F32 = jnp.float32
CHUNKS = 2
VMEM_KIB = 48 * 1024
ROWS = 32 // CHUNKS


def device(x, y, zh, zl, c):
    return (y * 4 + zh, x * 8 + zl * 2 + c)


def kernel(
    hist, free, start, now, out,
    start_s, now_s, hraw, htmp, h_all, fraw, ftmp, fpc, fa, fb, gsend, grecv, gsib, rsend, rrecv, xfin, pieces, otmp,
    lsem, hy_s, hy_r, hs_s, hs_r, f_s, f_r, g_s, g_r, gs_s, gs_r, r_s, r_r, az_s, az_r, ay_s, ay_r, known,
):
    mem, tt = lax.axis_index("mem"), lax.axis_index("tt")
    y, zh = mem // 4, mem % 4
    x, zl, c = tt // 8, (tt // 2) % 4, tt % 2
    sib = device(x, y, zh, zl, 1 - c)

    def remote(src, dst, ssem, rsem, dev):
        return pltpu.make_async_remote_copy(
            src_ref=src, dst_ref=dst, send_sem=ssem, recv_sem=rsem, device_id=dev, device_id_type=MESH
        )

    load_h = pltpu.make_async_copy(hist, hraw, lsem.at[0])
    load_f = pltpu.make_async_copy(free, fraw, lsem.at[1])
    load_s = pltpu.make_async_copy(start, start_s, lsem.at[2])
    load_n = pltpu.make_async_copy(now, now_s, lsem.at[3])
    load_h.start()
    load_f.start()
    load_s.start()
    load_n.start()

    def z_dev(d, core=c):
        z = (zh * 4 + zl + d + 16) % 16
        return device(x, y, z // 4, z % 4, core)

    def x_dev(d):
        return device((x + d) % 4, y, zh, zl, c)

    up, down, far = (y + 1) % 4, (y + 3) % 4, (y + 2) % 4
    up_dev, down_dev = device(x, up, zh, zl, c), device(x, down, zh, zl, c)

    def tell(sem, devs):
        for dev in devs:
            pl.semaphore_signal(sem, inc=1, device_id=dev, device_id_type=MESH)

    barrier = pltpu.get_barrier_semaphore()
    tell(barrier, (up_dev, down_dev, sib, x_dev(1), x_dev(3), z_dev(1), z_dev(-1)))

    load_f.wait()
    for part in range(2):
        for r in range(2):
            rows = pl.ds(pl.multiple_of(y * 64, 64), 64)
            ftmp[part, r] = fraw[part, r, rows, :].astype(F32)
    for part in range(2):
        for r in range(2):
            for t in range(2):
                for ch in range(CHUNKS):
                    at = pl.ds(ch * 2 * ROWS + t, ROWS, stride=2)
                    fpc[t, r, ch, part * ROWS : part * ROWS + ROWS, :] = ftmp[part, r, at, :].astype(BF16)

    load_h.wait()
    for sl in range(4):
        for part in range(2):
            htmp[sl, part] = hraw[part, sl].astype(F32)
        for part in range(2):
            for t in range(2):
                col = (t * 2 + part) * 128
                h_all[y, c, sl * 128 : sl * 128 + 128, col : col + 128] = htmp[
                    sl, part, pl.ds(t, 128, stride=2), :
                ].astype(BF16)

    pl.semaphore_wait(barrier, 7)
    tell(known.at[0], (x_dev(1), x_dev(3), z_dev(1), z_dev(-1)))
    sends = []

    def slab(b, core, sl):
        return h_all.at[b, core, pl.ds(sl * 128, 128), :]

    def hy(b, sl, k, dev):
        cp = remote(slab(b, c, sl), slab(b, c, sl), hy_s.at[k], hy_r.at[k], dev)
        cp.start()
        sends.append(cp)

    def hs(b, sl, k):
        cp = remote(slab(b, c, sl), slab(b, c, sl), hs_s.at[k], hs_r.at[k], sib)
        cp.start()
        sends.append(cp)

    def hy_wait(b, sl, k):
        remote(slab(b, c, sl), slab(b, c, sl), hy_s.at[k], hy_r.at[k], up_dev).wait_recv()

    for k in range(2):
        hy(y, k, k, up_dev)
        hy(y, k + 2, 4 + k, down_dev)
    for k in range(4):
        hs(y, k, k)

    pl.semaphore_wait(known.at[0], 4)
    tell(known.at[1], (z_dev(2), z_dev(-2)))

    load_s.wait()
    load_n.wait()
    pl.semaphore_wait(known.at[1], 2)
    tell(known.at[2], (z_dev(4), z_dev(-4)))
    tell(known.at[3], (x_dev(1), x_dev(3), x_dev(2)))

    for t in range(2):
        for r in range(2):
            to = 2 * c + t
            mine = (zl == to) & (c == r)

            @pl.when((zl == zh) & mine)
            def _():
                fa[...] = fpc[t, r]

            @pl.when((zl == zh) & jnp.logical_not(mine))
            def _():
                remote(fpc.at[t, r], fa, f_s.at[t * 2 + r], f_r.at[0], device(x, y, zh, to, r)).start()

    @pl.when(c == zh // 2)
    def _():
        for r in range(2):
            remote(fpc.at[zh % 2, r], fb, f_s.at[4 + r], f_r.at[1], z_dev(2, r)).start()

    for k in range(2):
        hy(y, k + 2, 2 + k, up_dev)
        hy(y, k, 6 + k, down_dev)
    pl.semaphore_wait(known.at[3], 3)
    for k in range(2):
        hy_wait(down, k, k)
        hy(down, k, 8 + k, up_dev)
        hs(down, k, 4 + k)
        hy_wait(up, k + 2, 4 + k)
        hy(up, k + 2, 10 + k, down_dev)
        hs(up, k + 2, 8 + k)

    @pl.when(jnp.logical_not((zl == zh) & (c == zl // 2)))
    def _():
        remote(fpc.at[0, 0], fa, f_s.at[0], f_r.at[0], sib).wait_recv()

    s_time = 16 * x + 4 * zh + zl
    live = jnp.where((start_s[c] <= s_time) & (s_time < now_s[0] + c), 1.0, 0.0).astype(F32)

    def gather(n, ch, value):
        re, im = value[:ROWS].astype(F32), value[ROWS:].astype(F32)
        mod = re * re + im * im
        gsend[n, ch, :ROWS, :] = (-(re * mod) * live).astype(BF16)
        gsend[n, ch, ROWS:, :] = (-(im * mod) * live).astype(BF16)
        for dx, dz in G_ORDER:
            dev = device((x + dx) % 4, y, zh, (zl + dz) % 4, c)
            cp = remote(gsend.at[n, ch], grecv.at[n, ch, x, zl], g_s.at[n, ch, dx * 4 + dz], g_r.at[n, ch, x, zl], dev)
            cp.start()
            sends.append(cp)
        grecv[n, ch, x, zl] = gsend[n, ch]

    def g_wait(n, ch, dx):
        for dz in range(4):
            if dx or dz:
                xs, zs = (x + dx) % 4, (zl + dz) % 4
                b = grecv.at[n, ch, xs, zs]
                remote(b, b, g_s.at[n, ch, 0], g_r.at[n, ch, xs, zs], sib).wait_recv()

    def product(n, ch, b, core):
        left = jnp.concatenate([grecv[n, ch, b, sl] for sl in range(4)], axis=1)
        return jnp.dot(left, h_all[b, core], preferred_element_type=F32)

    def r_block(n, ch, t, p):
        rsend[n, ch, t, :ROWS, :] = (p[:ROWS, :128] - p[ROWS:, 128:]).astype(BF16)
        rsend[n, ch, t, ROWS:, :] = (p[:ROWS, 128:] + p[ROWS:, :128]).astype(BF16)

    def multiply(n, ch):
        acc = [None, None]
        for d in (0, 1, 3, 2):
            g_wait(n, ch, d)
            for core in range(2):
                prod = product(n, ch, (x + d) % 4, core)
                acc[core] = prod if acc[core] is None else acc[core] + prod
        for t in range(4):
            r_block(n, ch, t, acc[t // 2][:, (t % 2) * 256 : (t % 2) * 256 + 256])

    def r_dest(n, t):
        if n == ITERS - 1 and n > 0:
            return z_dev(2 + 4 * (t - zh) + 16)
        if n > 0:
            return device(x, y, zl, t, c)
        return device(x, y, zl, 2 * c + t % 2, c if t < 2 else 1 - c)

    def r_here(n, t):
        if n == ITERS - 1 and n > 0:
            return False
        if n > 0:
            return (zh == zl) & (zl == t)
        return (zh == zl) & (zl == 2 * c + t % 2) if t < 2 else False

    def r_send(n, ch):
        for t in range(4):
            if r_here(n, t) is not False:

                @pl.when(r_here(n, t))
                def _():
                    rrecv[n, ch, zh] = rsend[n, ch, t]

            @pl.when(jnp.logical_not(r_here(n, t)))
            def _():
                remote(rsend.at[n, ch, t], rrecv.at[n, ch, zh], r_s.at[n, ch, t], r_r.at[n, ch, zh], r_dest(n, t)).start()

    def r_sum(n, ch, base):
        for src in range(4):
            if n == ITERS - 1 and n > 0:
                here = False
            elif n > 0:
                here = (zh == zl) & (zh == src)
            else:
                here = (zh == zl) & (zh == src) & (c == zl // 2)

            @pl.when(jnp.logical_not(here))
            def _():
                b = rrecv.at[n, ch, src]
                remote(b, b, r_s.at[n, ch, src], r_r.at[n, ch, src], sib).wait_recv()

        total = sum(rrecv[n, ch, src].astype(F32) for src in range(4))
        return (base[ch].astype(F32) + COUPLING * total).astype(BF16)

    def flush():
        for cp in sends:
            cp.wait_send()
        sends.clear()

    for ch in range(CHUNKS):
        gather(0, ch, fa[ch])

    for k in range(2):
        hy_wait(down, k + 2, 2 + k)
        hs(down, k + 2, 6 + k)
        hy_wait(up, k, 6 + k)
        hs(up, k, 10 + k)
    pl.semaphore_wait(known.at[2], 2)
    tell(known.at[4], (sib,))

    for ch in range(CHUNKS):
        for d in range(4):
            g_wait(0, ch, d)
        cp = remote(grecv.at[0, ch], gsib.at[ch], gs_s.at[ch], gs_r.at[ch], sib)
        cp.start()
        sends.append(cp)
    for ch in range(CHUNKS):
        remote(gsib.at[ch], gsib.at[ch], gs_s.at[ch], gs_r.at[ch], sib).wait_recv()

    def first(b):
        left = [[jnp.concatenate([g[b, sl] for sl in range(4)], axis=1) for g in (grecv.at[0, ch], gsib.at[ch])]
                for ch in range(CHUNKS)]
        return jnp.dot(jnp.concatenate(sum(left, []), axis=0), h_all[b, c], preferred_element_type=F32)

    acc = first(y) + first(down) + first(up)
    for k in range(2):
        hy_wait(far, k, 8 + k)
        hy_wait(far, k + 2, 10 + k)
    acc = acc + first(far)
    pl.semaphore_wait(known.at[4], 1)
    for ch in range(CHUNKS):
        for t in range(4):
            at = (ch * 2 + t // 2) * 2 * ROWS
            r_block(0, ch, t, acc[at : at + 2 * ROWS, (t % 2) * 256 : (t % 2) * 256 + 256])
        r_send(0, ch)
    for k in range(2):
        hs(far, k, 12 + k)
        hs(far, k + 2, 14 + k)
    for b, slabs in (
        (y, ((0, 0), (1, 1), (2, 2), (3, 3))),
        (down, ((0, 4), (1, 5), (2, 6), (3, 7))),
        (up, ((2, 8), (3, 9), (0, 10), (1, 11))),
        (far, ((0, 12), (1, 13), (2, 14), (3, 15))),
    ):
        for sl, k in slabs:
            remote(slab(b, 1 - c, sl), slab(b, 1 - c, sl), hs_s.at[k], hs_r.at[k], sib).wait_recv()

    for n in range(1, ITERS):
        flush()
        for ch in range(CHUNKS):
            gather(n, ch, r_sum(n - 1, ch, fa))
        for ch in range(CHUNKS):
            multiply(n, ch)
            r_send(n, ch)
    flush()

    remote(fpc.at[0, 0], fb, f_s.at[4], f_r.at[1], sib).wait_recv()

    block = (zh + 3 + zl // 2) % 4
    for ch in range(CHUNKS):
        xfin[ch] = r_sum(ITERS - 1, ch, fb)
        for k, d in enumerate((6, -6, 2, -2)):
            remote(
                xfin.at[ch], pieces.at[y, block % 2, c, ch], az_s.at[ch, k], az_r.at[block % 2, c, ch],
                z_dev(d, block // 2),
            ).start()

    near = jnp.where((2 * c - zh + 4) % 4 == 2, 1, 0)
    for order in range(2):
        t = near if order == 0 else 1 - near
        for ch in range(CHUNKS):
            for r in range(2):
                src = pieces.at[y, t, r, ch]

                remote(src, src, az_s.at[0, 0], az_r.at[t, r, ch], sib).wait_recv()
                for dy in (2, 1, 3):
                    k = (order * 2 + r) * CHUNKS + ch
                    dev = device(x, (y + dy) % 4, zh, zl, c)
                    cp = remote(src, src, ay_s.at[dy - 1, k], ay_r.at[y, t, r, ch], dev)
                    cp.start()
                    sends.append(cp)

    def assemble(b):
        for t in range(2):
            for r in range(2):
                for part in range(2):
                    for ch in range(CHUNKS):
                        at = pl.ds(pl.multiple_of(b * 64, 64) + ch * 2 * ROWS + t, ROWS, stride=2)
                        otmp[part, r, at, :] = pieces[b, t, r, ch, part * ROWS : part * ROWS + ROWS, :].astype(F32)
        for r in range(2):
            for part in range(2):
                rows = pl.ds(pl.multiple_of(b * 64, 64), 64)
                out[part, r, rows, :] = otmp[part, r, rows, :].astype(BF16)

    assemble(y)
    for dy in (1, 3, 2):
        b = (y + dy) % 4
        for t in range(2):
            for r in range(2):
                for ch in range(CHUNKS):
                    p = pieces.at[b, t, r, ch]
                    remote(p, p, ay_s.at[0, 0], ay_r.at[b, t, r, ch], sib).wait_recv()
        assemble(b)

    for t in range(2):
        for r in range(2):
            @pl.when((zl == zh) & jnp.logical_not((zl == 2 * c + t) & (c == r)))
            def _():
                remote(fpc.at[t, r], fa, f_s.at[t * 2 + r], f_r.at[0], sib).wait_send()

    @pl.when(c == zh // 2)
    def _():
        for r in range(2):
            remote(fpc.at[0, 0], fb, f_s.at[4 + r], f_r.at[1], sib).wait_send()

    for n in range(ITERS):
        for ch in range(CHUNKS):
            for t in range(4):
                @pl.when(jnp.logical_not(r_here(n, t)))
                def _():
                    b = rsend.at[n, ch, t]
                    remote(b, b, r_s.at[n, ch, t], r_r.at[n, ch, t], sib).wait_send()
    for ch in range(CHUNKS):
        for k in range(4):
            remote(xfin.at[ch], xfin.at[ch], az_s.at[ch, k], az_r.at[0, 0, ch], sib).wait_send()
    flush()


G_ORDER = tuple(
    sorted(
        ((dx, dz) for dx in range(4) for dz in range(4) if dx or dz),
        key=lambda d: -(min(d[0], 4 - d[0]) + min(d[1], 4 - d[1])),
    )
)


def on_device(history, free_rows, memory_start, now):
    vmem = pltpu.VMEM
    dma = pltpu.SemaphoreType.DMA
    block = (CHUNKS, 2 * ROWS, 128)
    result = pl.pallas_call(
        kernel,
        out_shape=jax.ShapeDtypeStruct((2, 2, 256, 128), BF16),
        in_specs=[pl.BlockSpec(memory_space=pltpu.HBM)] * 4,
        out_specs=pl.BlockSpec(memory_space=pltpu.VMEM),
        scratch_shapes=[
            pltpu.SMEM((2,), jnp.int32),
            pltpu.SMEM((1,), jnp.int32),
            vmem((2, 4, 256, 128), BF16),
            vmem((4, 2, 256, 128), F32),
            vmem((4, 2, 512, 512), BF16),
            vmem((2, 2, 256, 128), BF16),
            vmem((2, 2, 64, 128), F32),
            vmem((2, 2, *block), BF16),
            vmem(block, BF16),
            vmem(block, BF16),
            vmem((ITERS, *block), BF16),
            vmem((ITERS, CHUNKS, 4, 4, *block[1:]), BF16),
            vmem((CHUNKS, 4, 4, *block[1:]), BF16),
            vmem((ITERS, CHUNKS, 4, *block[1:]), BF16),
            vmem((ITERS, CHUNKS, 4, *block[1:]), BF16),
            vmem(block, BF16),
            vmem((4, 2, 2, *block), BF16),
            vmem((2, 2, 256, 128), F32),
            dma((4,)),
            dma((12,)), dma((12,)),
            dma((16,)), dma((16,)),
            dma((6,)), dma((2,)),
            dma((ITERS, CHUNKS, 16)), dma((ITERS, CHUNKS, 4, 4)),
            dma((CHUNKS,)), dma((CHUNKS,)),
            dma((ITERS, CHUNKS, 4)), dma((ITERS, CHUNKS, 4)),
            dma((CHUNKS, 4)), dma((2, 2, CHUNKS)),
            dma((3, 4 * CHUNKS)), dma((4, 2, 2, CHUNKS)),
            pltpu.SemaphoreType.REGULAR((5,)),
        ],
        compiler_params=pltpu.CompilerParams(
            collective_id=0, has_side_effects=True, vmem_limit_bytes=VMEM_KIB * 1024
        ),
        name="fixed_point",
    )(
        *(
            pltpu.with_memory_space_constraint(array, pltpu.HBM)
            for array in (history.reshape(2, 4, 256, 128), free_rows.reshape(2, 2, 256, 128), memory_start)
        ),
        now,
    )
    return result.reshape(free_rows.shape)


def solution(mesh):
    return jax.shard_map(
        on_device,
        mesh=mesh,
        in_specs=(P(None, "mem", None, "tt", None), P(None, None, None, "tt", None), P(), P()),
        out_specs=P(None, None, None, "tt", None),
        check_vma=False,
    )
```

```python
import functools

import jax
import jax.numpy as jnp
from jax import lax
from jax.experimental import pallas as pl
from jax.experimental.pallas import tpu as pltpu
from jax.sharding import PartitionSpec as P

ITERS = 3
COUPLING = 0.5
MESH = pl.DeviceIdType.MESH
BF16 = jnp.bfloat16
F32 = jnp.float32
CHUNKS = 2
VMEM_KIB = 48 * 1024
ROWS = 32 // CHUNKS


def device(x, y, zh, zl, c):
    return (y * 4 + zh, x * 8 + zl * 2 + c)


def kernel(
    hist, free, start, now, out,
    start_s, now_s, hraw, htmp, h_all, fraw, ftmp, fpc, fa, fb, gsend, grecv, gsib, rsend, rrecv, xfin, pieces, otmp,
    lsem, hy_s, hy_r, hs_s, hs_r, f_s, f_r, g_s, g_r, gs_s, gs_r, r_s, r_r, az_s, az_r, ay_s, ay_r, known,
):
    mem, tt = lax.axis_index("mem"), lax.axis_index("tt")
    y, zh = mem // 4, mem % 4
    x, zl, c = tt // 8, (tt // 2) % 4, tt % 2
    sib = device(x, y, zh, zl, 1 - c)

    def remote(src, dst, ssem, rsem, dev):
        return pltpu.make_async_remote_copy(
            src_ref=src, dst_ref=dst, send_sem=ssem, recv_sem=rsem, device_id=dev, device_id_type=MESH
        )

    load_h = pltpu.make_async_copy(hist, hraw, lsem.at[0])
    load_f = pltpu.make_async_copy(free, fraw, lsem.at[1])
    load_s = pltpu.make_async_copy(start, start_s, lsem.at[2])
    load_n = pltpu.make_async_copy(now, now_s, lsem.at[3])
    load_h.start()
    load_f.start()
    load_s.start()
    load_n.start()

    def z_dev(d, core=c):
        z = (zh * 4 + zl + d + 16) % 16
        return device(x, y, z // 4, z % 4, core)

    def x_dev(d):
        return device((x + d) % 4, y, zh, zl, c)

    up, down, far = (y + 1) % 4, (y + 3) % 4, (y + 2) % 4
    up_dev, down_dev = device(x, up, zh, zl, c), device(x, down, zh, zl, c)

    def tell(sem, devs):
        for dev in devs:
            pl.semaphore_signal(sem, inc=1, device_id=dev, device_id_type=MESH)

    barrier = pltpu.get_barrier_semaphore()
    tell(barrier, (up_dev, down_dev, sib, x_dev(1), x_dev(3), z_dev(1), z_dev(-1)))

    load_f.wait()
    for part in range(2):
        for r in range(2):
            rows = pl.ds(pl.multiple_of(y * 64, 64), 64)
            ftmp[part, r] = fraw[part, r, rows, :].astype(F32)
    for part in range(2):
        for r in range(2):
            for t in range(2):
                for ch in range(CHUNKS):
                    at = pl.ds(ch * 2 * ROWS + t, ROWS, stride=2)
                    fpc[t, r, ch, part * ROWS : part * ROWS + ROWS, :] = ftmp[part, r, at, :].astype(BF16)

    load_h.wait()
    for sl in range(4):
        for part in range(2):
            htmp[sl, part] = hraw[part, sl].astype(F32)
        for part in range(2):
            for t in range(2):
                col = (t * 2 + part) * 128
                h_all[y, c, sl * 128 : sl * 128 + 128, col : col + 128] = htmp[
                    sl, part, pl.ds(t, 128, stride=2), :
                ].astype(BF16)

    pl.semaphore_wait(barrier, 7)
    tell(known.at[0], (x_dev(1), x_dev(3), z_dev(1), z_dev(-1)))
    sends, gathers = [], []
    fifteen = h_all.at[0, 0, pl.ds(0, 15 * 2 * ROWS), pl.ds(0, 128)]

    def slab(b, core, sl):
        return h_all.at[b, core, pl.ds(sl * 128, 128), :]

    def hy(b, sl, k, dev):
        cp = remote(slab(b, c, sl), slab(b, c, sl), hy_s.at[k], hy_r.at[k], dev)
        cp.start()
        sends.append(cp)

    def hs(b, sl, k):
        cp = remote(slab(b, c, sl), slab(b, c, sl), hs_s.at[k], hs_r.at[k], sib)
        cp.start()
        sends.append(cp)

    def hy_wait(b, sl, k):
        remote(slab(b, c, sl), slab(b, c, sl), hy_s.at[k], hy_r.at[k], up_dev).wait_recv()

    for k in range(2):
        hy(y, k, k, up_dev)
        hy(y, k + 2, 4 + k, down_dev)
    for k in range(4):
        hs(y, k, k)

    pl.semaphore_wait(known.at[0], 4)
    tell(known.at[1], (z_dev(2), z_dev(-2)))

    load_s.wait()
    load_n.wait()
    pl.semaphore_wait(known.at[1], 2)
    tell(known.at[2], (z_dev(4), z_dev(-4)))
    tell(known.at[3], (x_dev(1), x_dev(3), x_dev(2)))

    for t in range(2):
        for r in range(2):
            to = 2 * c + t
            mine = (zl == to) & (c == r)

            @pl.when((zl == zh) & mine)
            def _():
                fa[...] = fpc[t, r]

            @pl.when((zl == zh) & jnp.logical_not(mine))
            def _():
                remote(fpc.at[t, r], fa, f_s.at[t * 2 + r], f_r.at[0], device(x, y, zh, to, r)).start()

    @pl.when(c == zh // 2)
    def _():
        for r in range(2):
            remote(fpc.at[zh % 2, r], fb, f_s.at[4 + r], f_r.at[1], z_dev(2, r)).start()

    for k in range(2):
        hy(y, k + 2, 2 + k, up_dev)
        hy(y, k, 6 + k, down_dev)
    pl.semaphore_wait(known.at[3], 3)
    for k in range(2):
        hy_wait(down, k, k)
        hy(down, k, 8 + k, up_dev)
        hs(down, k, 4 + k)
        hy_wait(up, k + 2, 4 + k)
        hy(up, k + 2, 10 + k, down_dev)
        hs(up, k + 2, 8 + k)

    @pl.when(jnp.logical_not((zl == zh) & (c == zl // 2)))
    def _():
        remote(fpc.at[0, 0], fa, f_s.at[0], f_r.at[0], sib).wait_recv()

    s_time = 16 * x + 4 * zh + zl
    live = jnp.where((start_s[c] <= s_time) & (s_time < now_s[0] + c), 1.0, 0.0).astype(F32)

    def gather(n, ch, value):
        re, im = value[:ROWS].astype(F32), value[ROWS:].astype(F32)
        mod = re * re + im * im
        gsend[n, ch, :ROWS, :] = (-(re * mod) * live).astype(BF16)
        gsend[n, ch, ROWS:, :] = (-(im * mod) * live).astype(BF16)
        for dx, dz in G_ORDER:
            dev = device((x + dx) % 4, y, zh, (zl + dz) % 4, c)
            remote(gsend.at[n, ch], grecv.at[n, ch, x, zl], g_s.at[n, ch], g_r.at[n, ch, (4 - dx) % 4], dev).start()
        gathers.append((n, ch))
        grecv[n, ch, x, zl] = gsend[n, ch]

    def g_wait(n, ch, dx):
        b = grecv.at[n, ch, (x + dx) % 4, pl.ds(0, 4 if dx else 3)]
        remote(b, b, g_s.at[n, ch], g_r.at[n, ch, dx], sib).wait_recv()

    def product(n, ch, b, core):
        left = jnp.concatenate([grecv[n, ch, b, sl] for sl in range(4)], axis=1)
        return jnp.dot(left, h_all[b, core], preferred_element_type=F32)

    def r_block(n, ch, t, p):
        rsend[n, ch, t, :ROWS, :] = (p[:ROWS, :128] - p[ROWS:, 128:]).astype(BF16)
        rsend[n, ch, t, ROWS:, :] = (p[:ROWS, 128:] + p[ROWS:, :128]).astype(BF16)

    def multiply(n, ch):
        acc = [None, None]
        for d in (0, 1, 3, 2):
            g_wait(n, ch, d)
            for core in range(2):
                prod = product(n, ch, (x + d) % 4, core)
                acc[core] = prod if acc[core] is None else acc[core] + prod
        for t in range(4):
            r_block(n, ch, t, acc[t // 2][:, (t % 2) * 256 : (t % 2) * 256 + 256])

    def r_dest(n, t):
        if n == ITERS - 1 and n > 0:
            return z_dev(2 + 4 * (t - zh) + 16)
        if n > 0:
            return device(x, y, zl, t, c)
        return device(x, y, zl, 2 * c + t % 2, c if t < 2 else 1 - c)

    def r_here(n, t):
        if n == ITERS - 1 and n > 0:
            return False
        if n > 0:
            return (zh == zl) & (zl == t)
        return (zh == zl) & (zl == 2 * c + t % 2) if t < 2 else False

    def r_send(n, ch):
        for t in range(4):
            if r_here(n, t) is not False:

                @pl.when(r_here(n, t))
                def _():
                    rrecv[n, ch, zh] = rsend[n, ch, t]

            @pl.when(jnp.logical_not(r_here(n, t)))
            def _():
                remote(rsend.at[n, ch, t], rrecv.at[n, ch, zh], r_s.at[n, ch, t], r_r.at[n, ch, zh], r_dest(n, t)).start()

    def r_sum(n, ch, base):
        for src in range(4):
            if n == ITERS - 1 and n > 0:
                here = False
            elif n > 0:
                here = (zh == zl) & (zh == src)
            else:
                here = (zh == zl) & (zh == src) & (c == zl // 2)

            @pl.when(jnp.logical_not(here))
            def _():
                b = rrecv.at[n, ch, src]
                remote(b, b, r_s.at[n, ch, src], r_r.at[n, ch, src], sib).wait_recv()

        total = sum(rrecv[n, ch, src].astype(F32) for src in range(4))
        return (base[ch].astype(F32) + COUPLING * total).astype(BF16)

    def flush():
        for cp in sends:
            cp.wait_send()
        sends.clear()
        for n, ch in gathers:
            b = fifteen
            remote(b, b, g_s.at[n, ch], g_r.at[n, ch, 0], sib).wait_send()
        gathers.clear()

    for ch in range(CHUNKS):
        gather(0, ch, fa[ch])

    for k in range(2):
        hy_wait(down, k + 2, 2 + k)
        hs(down, k + 2, 6 + k)
        hy_wait(up, k, 6 + k)
        hs(up, k, 10 + k)
    pl.semaphore_wait(known.at[2], 2)
    tell(known.at[4], (sib,))

    for ch in range(CHUNKS):
        for d in range(4):
            g_wait(0, ch, d)
        cp = remote(grecv.at[0, ch], gsib.at[ch], gs_s.at[ch], gs_r.at[ch], sib)
        cp.start()
        sends.append(cp)
    for ch in range(CHUNKS):
        remote(gsib.at[ch], gsib.at[ch], gs_s.at[ch], gs_r.at[ch], sib).wait_recv()

    def first(b):
        left = [[jnp.concatenate([g[b, sl] for sl in range(4)], axis=1) for g in (grecv.at[0, ch], gsib.at[ch])]
                for ch in range(CHUNKS)]
        return jnp.dot(jnp.concatenate(sum(left, []), axis=0), h_all[b, c], preferred_element_type=F32)

    acc = first(y) + first(down) + first(up)
    for k in range(2):
        hy_wait(far, k, 8 + k)
        hy_wait(far, k + 2, 10 + k)
    acc = acc + first(far)
    pl.semaphore_wait(known.at[4], 1)
    for ch in range(CHUNKS):
        for t in range(4):
            at = (ch * 2 + t // 2) * 2 * ROWS
            r_block(0, ch, t, acc[at : at + 2 * ROWS, (t % 2) * 256 : (t % 2) * 256 + 256])
        r_send(0, ch)
    for k in range(2):
        hs(far, k, 12 + k)
        hs(far, k + 2, 14 + k)
    for b, slabs in (
        (y, ((0, 0), (1, 1), (2, 2), (3, 3))),
        (down, ((0, 4), (1, 5), (2, 6), (3, 7))),
        (up, ((2, 8), (3, 9), (0, 10), (1, 11))),
        (far, ((0, 12), (1, 13), (2, 14), (3, 15))),
    ):
        for sl, k in slabs:
            remote(slab(b, 1 - c, sl), slab(b, 1 - c, sl), hs_s.at[k], hs_r.at[k], sib).wait_recv()

    for n in range(1, ITERS):
        flush()
        for ch in range(CHUNKS):
            gather(n, ch, r_sum(n - 1, ch, fa))
        for ch in range(CHUNKS):
            multiply(n, ch)
            r_send(n, ch)
    flush()

    remote(fpc.at[0, 0], fb, f_s.at[4], f_r.at[1], sib).wait_recv()

    block = (zh + 3 + zl // 2) % 4
    for ch in range(CHUNKS):
        xfin[ch] = r_sum(ITERS - 1, ch, fb)
        for k, d in enumerate((6, -6, 2, -2)):
            remote(
                xfin.at[ch], pieces.at[y, block % 2, c, ch], az_s.at[ch, k], az_r.at[block % 2, c, ch],
                z_dev(d, block // 2),
            ).start()

    near = jnp.where((2 * c - zh + 4) % 4 == 2, 1, 0)
    for order in range(2):
        t = near if order == 0 else 1 - near
        for ch in range(CHUNKS):
            for r in range(2):
                src = pieces.at[y, t, r, ch]

                remote(src, src, az_s.at[0, 0], az_r.at[t, r, ch], sib).wait_recv()
                for dy in (2, 1, 3):
                    dev = device(x, (y + dy) % 4, zh, zl, c)
                    remote(src, src, ay_s.at[dy - 1], ay_r.at[y], dev).start()

    def assemble(b):
        for t in range(2):
            for r in range(2):
                for part in range(2):
                    for ch in range(CHUNKS):
                        at = pl.ds(pl.multiple_of(b * 64, 64) + ch * 2 * ROWS + t, ROWS, stride=2)
                        otmp[part, r, at, :] = pieces[b, t, r, ch, part * ROWS : part * ROWS + ROWS, :].astype(F32)
        for r in range(2):
            for part in range(2):
                rows = pl.ds(pl.multiple_of(b * 64, 64), 64)
                out[part, r, rows, :] = otmp[part, r, rows, :].astype(BF16)

    assemble(y)
    for dy in (1, 3, 2):
        b = (y + dy) % 4
        remote(pieces.at[b], pieces.at[b], ay_s.at[0], ay_r.at[b], sib).wait_recv()
        assemble(b)

    for t in range(2):
        for r in range(2):
            @pl.when((zl == zh) & jnp.logical_not((zl == 2 * c + t) & (c == r)))
            def _():
                remote(fpc.at[t, r], fa, f_s.at[t * 2 + r], f_r.at[0], sib).wait_send()

    @pl.when(c == zh // 2)
    def _():
        for r in range(2):
            remote(fpc.at[0, 0], fb, f_s.at[4 + r], f_r.at[1], sib).wait_send()

    for n in range(ITERS):
        for ch in range(CHUNKS):
            for t in range(4):
                @pl.when(jnp.logical_not(r_here(n, t)))
                def _():
                    b = rsend.at[n, ch, t]
                    remote(b, b, r_s.at[n, ch, t], r_r.at[n, ch, t], sib).wait_send()
    for ch in range(CHUNKS):
        for k in range(4):
            remote(xfin.at[ch], xfin.at[ch], az_s.at[ch, k], az_r.at[0, 0, ch], sib).wait_send()
    flush()
    for dy in range(1, 4):
        remote(pieces.at[0], pieces.at[0], ay_s.at[dy - 1], ay_r.at[0], sib).wait_send()


G_ORDER = tuple(
    sorted(
        ((dx, dz) for dx in range(4) for dz in range(4) if dx or dz),
        key=lambda d: -(min(d[0], 4 - d[0]) + min(d[1], 4 - d[1])),
    )
)


def on_device(history, free_rows, memory_start, now):
    vmem = pltpu.VMEM
    dma = pltpu.SemaphoreType.DMA
    block = (CHUNKS, 2 * ROWS, 128)
    result = pl.pallas_call(
        kernel,
        out_shape=jax.ShapeDtypeStruct((2, 2, 256, 128), BF16),
        in_specs=[pl.BlockSpec(memory_space=pltpu.HBM)] * 4,
        out_specs=pl.BlockSpec(memory_space=pltpu.VMEM),
        scratch_shapes=[
            pltpu.SMEM((2,), jnp.int32),
            pltpu.SMEM((1,), jnp.int32),
            vmem((2, 4, 256, 128), BF16),
            vmem((4, 2, 256, 128), F32),
            vmem((4, 2, 512, 512), BF16),
            vmem((2, 2, 256, 128), BF16),
            vmem((2, 2, 64, 128), F32),
            vmem((2, 2, *block), BF16),
            vmem(block, BF16),
            vmem(block, BF16),
            vmem((ITERS, *block), BF16),
            vmem((ITERS, CHUNKS, 4, 4, *block[1:]), BF16),
            vmem((CHUNKS, 4, 4, *block[1:]), BF16),
            vmem((ITERS, CHUNKS, 4, *block[1:]), BF16),
            vmem((ITERS, CHUNKS, 4, *block[1:]), BF16),
            vmem(block, BF16),
            vmem((4, 2, 2, *block), BF16),
            vmem((2, 2, 256, 128), F32),
            dma((4,)),
            dma((12,)), dma((12,)),
            dma((16,)), dma((16,)),
            dma((6,)), dma((2,)),
            dma((ITERS, CHUNKS)), dma((ITERS, CHUNKS, 4)),
            dma((CHUNKS,)), dma((CHUNKS,)),
            dma((ITERS, CHUNKS, 4)), dma((ITERS, CHUNKS, 4)),
            dma((CHUNKS, 4)), dma((2, 2, CHUNKS)),
            dma((3,)), dma((4,)),
            pltpu.SemaphoreType.REGULAR((5,)),
        ],
        compiler_params=pltpu.CompilerParams(
            collective_id=0, has_side_effects=True, vmem_limit_bytes=VMEM_KIB * 1024
        ),
        name="fixed_point",
    )(
        *(
            pltpu.with_memory_space_constraint(array, pltpu.HBM)
            for array in (history.reshape(2, 4, 256, 128), free_rows.reshape(2, 2, 256, 128), memory_start)
        ),
        now,
    )
    return result.reshape(free_rows.shape)


def solution(mesh):
    return jax.shard_map(
        on_device,
        mesh=mesh,
        in_specs=(P(None, "mem", None, "tt", None), P(None, None, None, "tt", None), P(), P()),
        out_specs=P(None, None, None, "tt", None),
        check_vma=False,
    )
```

```python
import functools

import jax
import jax.numpy as jnp
from jax import lax
from jax.experimental import pallas as pl
from jax.experimental.pallas import tpu as pltpu
from jax.sharding import PartitionSpec as P

ITERS = 3
COUPLING = 0.5
MESH = pl.DeviceIdType.MESH
BF16 = jnp.bfloat16
F32 = jnp.float32
CHUNKS = 2
VMEM_KIB = 48 * 1024
ROWS = 32 // CHUNKS


def device(x, y, zh, zl, c):
    return (y * 4 + zh, x * 8 + zl * 2 + c)


def kernel(
    hist, free, start, now, out,
    start_s, now_s, hraw, htmp, h_all, fraw, ftmp, fpc, fa, fb, gsend, grecv, gsib, rsend, rrecv, xfin, pieces, otmp,
    lsem, hy_s, hy_r, hs_s, hs_r, f_s, f_r, g_s, g_r, gs_s, gs_r, r_s, r_r, az_s, az_r, ay_s, ay_r, known,
):
    mem, tt = lax.axis_index("mem"), lax.axis_index("tt")
    y, zh = mem // 4, mem % 4
    x, zl, c = tt // 8, (tt // 2) % 4, tt % 2
    sib = device(x, y, zh, zl, 1 - c)

    def remote(src, dst, ssem, rsem, dev):
        return pltpu.make_async_remote_copy(
            src_ref=src, dst_ref=dst, send_sem=ssem, recv_sem=rsem, device_id=dev, device_id_type=MESH
        )

    load_h = pltpu.make_async_copy(hist, hraw, lsem.at[0])
    load_f = pltpu.make_async_copy(free, fraw, lsem.at[1])
    load_s = pltpu.make_async_copy(start, start_s, lsem.at[2])
    load_n = pltpu.make_async_copy(now, now_s, lsem.at[3])
    load_h.start()
    load_f.start()
    load_s.start()
    load_n.start()

    def z_dev(d, core=c):
        z = (zh * 4 + zl + d + 16) % 16
        return device(x, y, z // 4, z % 4, core)

    def x_dev(d):
        return device((x + d) % 4, y, zh, zl, c)

    up, down, far = (y + 1) % 4, (y + 3) % 4, (y + 2) % 4
    up_dev, down_dev = device(x, up, zh, zl, c), device(x, down, zh, zl, c)

    def tell(sem, devs):
        for dev in devs:
            pl.semaphore_signal(sem, inc=1, device_id=dev, device_id_type=MESH)

    barrier = pltpu.get_barrier_semaphore()
    tell(barrier, (up_dev, down_dev, sib, x_dev(1), x_dev(3), z_dev(1), z_dev(-1)))

    load_f.wait()
    for part in range(2):
        for r in range(2):
            rows = pl.ds(pl.multiple_of(y * 64, 64), 64)
            ftmp[part, r] = fraw[part, r, rows, :].astype(F32)
    for part in range(2):
        for r in range(2):
            for t in range(2):
                for ch in range(CHUNKS):
                    at = pl.ds(ch * 2 * ROWS + t, ROWS, stride=2)
                    fpc[t, r, ch, part * ROWS : part * ROWS + ROWS, :] = ftmp[part, r, at, :].astype(BF16)

    load_h.wait()
    for sl in range(4):
        for part in range(2):
            htmp[sl, part] = hraw[part, sl].astype(F32)
        for part in range(2):
            for t in range(2):
                col = (t * 2 + part) * 128
                h_all[y, c, sl * 128 : sl * 128 + 128, col : col + 128] = htmp[
                    sl, part, pl.ds(t, 128, stride=2), :
                ].astype(BF16)

    pl.semaphore_wait(barrier, 7)
    tell(known.at[0], (x_dev(1), x_dev(3), z_dev(1), z_dev(-1)))
    sends, gathers = [], []
    fifteen = h_all.at[0, 0, pl.ds(0, 15 * 2 * ROWS), pl.ds(0, 128)]

    def slab(b, core, sl):
        return h_all.at[b, core, pl.ds(sl * 128, 128), :]

    def hy(b, sl, k, dev):
        cp = remote(slab(b, c, sl), slab(b, c, sl), hy_s.at[k], hy_r.at[k], dev)
        cp.start()
        sends.append(cp)

    def hs(b, sl, k):
        cp = remote(slab(b, c, sl), slab(b, c, sl), hs_s.at[k], hs_r.at[k], sib)
        cp.start()
        sends.append(cp)

    def hy_wait(b, sl, k):
        remote(slab(b, c, sl), slab(b, c, sl), hy_s.at[k], hy_r.at[k], up_dev).wait_recv()

    for k in range(2):
        hy(y, k, k, up_dev)
        hy(y, k + 2, 4 + k, down_dev)
    for k in range(4):
        hs(y, k, k)

    pl.semaphore_wait(known.at[0], 4)
    tell(known.at[1], (z_dev(2), z_dev(-2)))

    load_s.wait()
    load_n.wait()
    pl.semaphore_wait(known.at[1], 2)
    tell(known.at[2], (z_dev(4), z_dev(-4)))
    tell(known.at[3], (x_dev(1), x_dev(3), x_dev(2)))

    for t in range(2):
        for r in range(2):
            to = 2 * c + t
            mine = (zl == to) & (c == r)

            @pl.when((zl == zh) & mine)
            def _():
                fa[...] = fpc[t, r]

            @pl.when((zl == zh) & jnp.logical_not(mine))
            def _():
                remote(fpc.at[t, r], fa, f_s.at[t * 2 + r], f_r.at[0], device(x, y, zh, to, r)).start()

    @pl.when(c == zh // 2)
    def _():
        for r in range(2):
            remote(fpc.at[zh % 2, r], fb, f_s.at[4 + r], f_r.at[1], z_dev(2, r)).start()

    for k in range(2):
        hy(y, k + 2, 2 + k, up_dev)
        hy(y, k, 6 + k, down_dev)
    pl.semaphore_wait(known.at[3], 3)
    for k in range(2):
        hy_wait(down, k, k)
        hy(down, k, 8 + k, up_dev)
        hs(down, k, 4 + k)
        hy_wait(up, k + 2, 4 + k)
        hy(up, k + 2, 10 + k, down_dev)
        hs(up, k + 2, 8 + k)

    @pl.when(jnp.logical_not((zl == zh) & (c == zl // 2)))
    def _():
        remote(fpc.at[0, 0], fa, f_s.at[0], f_r.at[0], sib).wait_recv()

    s_time = 16 * x + 4 * zh + zl
    live = jnp.where((start_s[c] <= s_time) & (s_time < now_s[0] + c), 1.0, 0.0).astype(F32)

    def gather(n, ch, value):
        re, im = value[:ROWS].astype(F32), value[ROWS:].astype(F32)
        mod = re * re + im * im
        gsend[n, ch, :ROWS, :] = (-(re * mod) * live).astype(BF16)
        gsend[n, ch, ROWS:, :] = (-(im * mod) * live).astype(BF16)
        for dx, dz in G_ORDER:
            dev = device((x + dx) % 4, y, zh, (zl + dz) % 4, c)
            remote(gsend.at[n, ch], grecv.at[n, ch, x, zl], g_s.at[n, ch], g_r.at[n, ch, (4 - dx) % 4], dev).start()
        gathers.append((n, ch))
        grecv[n, ch, x, zl] = gsend[n, ch]

    def g_wait(n, ch, dx):
        b = grecv.at[n, ch, (x + dx) % 4, pl.ds(0, 4 if dx else 3)]
        remote(b, b, g_s.at[n, ch], g_r.at[n, ch, dx], sib).wait_recv()

    def product(n, ch, b, core):
        left = jnp.concatenate([grecv[n, ch, b, sl] for sl in range(4)], axis=1)
        return jnp.dot(left, h_all[b, core], preferred_element_type=F32)

    def r_block(n, ch, t, p):
        rsend[n, ch, t, :ROWS, :] = (p[:ROWS, :128] - p[ROWS:, 128:]).astype(BF16)
        rsend[n, ch, t, ROWS:, :] = (p[:ROWS, 128:] + p[ROWS:, :128]).astype(BF16)

    def multiply(n, ch):
        acc = [None, None]
        for d in (0, 1, 3, 2):
            g_wait(n, ch, d)
            for core in range(2):
                prod = product(n, ch, (x + d) % 4, core)
                acc[core] = prod if acc[core] is None else acc[core] + prod
        for t in range(4):
            r_block(n, ch, t, acc[t // 2][:, (t % 2) * 256 : (t % 2) * 256 + 256])

    def r_dest(n, t):
        if n == ITERS - 1 and n > 0:
            return z_dev(2 + 4 * (t - zh) + 16)
        if n > 0:
            return device(x, y, zl, t, c)
        return device(x, y, zl, 2 * c + t % 2, c if t < 2 else 1 - c)

    def r_here(n, t):
        if n == ITERS - 1 and n > 0:
            return False
        if n > 0:
            return (zh == zl) & (zl == t)
        return (zh == zl) & (zl == 2 * c + t % 2) if t < 2 else False

    def r_send(n, ch):
        for t in range(4):
            if r_here(n, t) is not False:

                @pl.when(r_here(n, t))
                def _():
                    rrecv[n, ch, zh] = rsend[n, ch, t]

            @pl.when(jnp.logical_not(r_here(n, t)))
            def _():
                remote(rsend.at[n, ch, t], rrecv.at[n, ch, zh], r_s.at[n, ch, t], r_r.at[n, ch], r_dest(n, t)).start()

    def r_sum(n, ch, base):
        b = rrecv.at[n, ch]
        if n == ITERS - 1 and n > 0:
            remote(b, b, r_s.at[n, ch, 0], r_r.at[n, ch], sib).wait_recv()
        else:
            here = (zh == zl) if n > 0 else (zh == zl) & (c == zl // 2)

            @pl.when(here)
            def _():
                three = rrecv.at[n, ch, pl.ds(0, 3)]
                remote(three, three, r_s.at[n, ch, 0], r_r.at[n, ch], sib).wait_recv()

            @pl.when(jnp.logical_not(here))
            def _():
                remote(b, b, r_s.at[n, ch, 0], r_r.at[n, ch], sib).wait_recv()

        total = sum(rrecv[n, ch, src].astype(F32) for src in range(4))
        return (base[ch].astype(F32) + COUPLING * total).astype(BF16)

    def flush():
        for cp in sends:
            cp.wait_send()
        sends.clear()
        for n, ch in gathers:
            b = fifteen
            remote(b, b, g_s.at[n, ch], g_r.at[n, ch, 0], sib).wait_send()
        gathers.clear()

    for ch in range(CHUNKS):
        gather(0, ch, fa[ch])

    for k in range(2):
        hy_wait(down, k + 2, 2 + k)
        hs(down, k + 2, 6 + k)
        hy_wait(up, k, 6 + k)
        hs(up, k, 10 + k)
    pl.semaphore_wait(known.at[2], 2)
    tell(known.at[4], (sib,))

    for ch in range(CHUNKS):
        for d in range(4):
            g_wait(0, ch, d)
        cp = remote(grecv.at[0, ch], gsib.at[ch], gs_s.at[ch], gs_r.at[ch], sib)
        cp.start()
        sends.append(cp)
    for ch in range(CHUNKS):
        remote(gsib.at[ch], gsib.at[ch], gs_s.at[ch], gs_r.at[ch], sib).wait_recv()

    def first(b):
        left = [[jnp.concatenate([g[b, sl] for sl in range(4)], axis=1) for g in (grecv.at[0, ch], gsib.at[ch])]
                for ch in range(CHUNKS)]
        return jnp.dot(jnp.concatenate(sum(left, []), axis=0), h_all[b, c], preferred_element_type=F32)

    acc = first(y) + first(down) + first(up)
    for k in range(2):
        hy_wait(far, k, 8 + k)
        hy_wait(far, k + 2, 10 + k)
    acc = acc + first(far)
    pl.semaphore_wait(known.at[4], 1)
    for ch in range(CHUNKS):
        for t in range(4):
            at = (ch * 2 + t // 2) * 2 * ROWS
            r_block(0, ch, t, acc[at : at + 2 * ROWS, (t % 2) * 256 : (t % 2) * 256 + 256])
        r_send(0, ch)
    for k in range(2):
        hs(far, k, 12 + k)
        hs(far, k + 2, 14 + k)
    for b, slabs in (
        (y, ((0, 0), (1, 1), (2, 2), (3, 3))),
        (down, ((0, 4), (1, 5), (2, 6), (3, 7))),
        (up, ((2, 8), (3, 9), (0, 10), (1, 11))),
        (far, ((0, 12), (1, 13), (2, 14), (3, 15))),
    ):
        for sl, k in slabs:
            remote(slab(b, 1 - c, sl), slab(b, 1 - c, sl), hs_s.at[k], hs_r.at[k], sib).wait_recv()

    for n in range(1, ITERS):
        flush()
        for ch in range(CHUNKS):
            gather(n, ch, r_sum(n - 1, ch, fa))
        for ch in range(CHUNKS):
            multiply(n, ch)
            r_send(n, ch)
    flush()

    remote(fpc.at[0, 0], fb, f_s.at[4], f_r.at[1], sib).wait_recv()

    block = (zh + 3 + zl // 2) % 4
    for ch in range(CHUNKS):
        xfin[ch] = r_sum(ITERS - 1, ch, fb)
        for k, d in enumerate((6, -6, 2, -2)):
            remote(
                xfin.at[ch], pieces.at[y, block % 2, ch, c], az_s.at[ch, k], az_r.at[block % 2, ch],
                z_dev(d, block // 2),
            ).start()

    for t in range(2):
        for r in range(2):
            @pl.when((zl == zh) & jnp.logical_not((zl == 2 * c + t) & (c == r)))
            def _():
                remote(fpc.at[t, r], fa, f_s.at[t * 2 + r], f_r.at[0], sib).wait_send()

    @pl.when(c == zh // 2)
    def _():
        for r in range(2):
            remote(fpc.at[0, 0], fb, f_s.at[4 + r], f_r.at[1], sib).wait_send()

    for n in range(ITERS):
        for ch in range(CHUNKS):
            for t in range(4):
                @pl.when(jnp.logical_not(r_here(n, t)))
                def _():
                    b = rsend.at[n, ch, t]
                    remote(b, b, r_s.at[n, ch, t], r_r.at[n, ch], sib).wait_send()

    near = jnp.where((2 * c - zh + 4) % 4 == 2, 1, 0)
    for order in range(2):
        t = near if order == 0 else 1 - near
        for ch in range(CHUNKS):
            src = pieces.at[y, t, ch]
            remote(src, src, az_s.at[0, 0], az_r.at[t, ch], sib).wait_recv()
            for dy in (2, 1, 3):
                dev = device(x, (y + dy) % 4, zh, zl, c)
                remote(src, src, ay_s.at[dy - 1], ay_r.at[y], dev).start()

    def assemble(b):
        for t in range(2):
            for r in range(2):
                for part in range(2):
                    for ch in range(CHUNKS):
                        at = pl.ds(pl.multiple_of(b * 64, 64) + ch * 2 * ROWS + t, ROWS, stride=2)
                        otmp[part, r, at, :] = pieces[b, t, ch, r, part * ROWS : part * ROWS + ROWS, :].astype(F32)
        for r in range(2):
            for part in range(2):
                rows = pl.ds(pl.multiple_of(b * 64, 64), 64)
                out[part, r, rows, :] = otmp[part, r, rows, :].astype(BF16)

    assemble(y)
    for dy in (1, 3, 2):
        b = (y + dy) % 4
        remote(pieces.at[b], pieces.at[b], ay_s.at[0], ay_r.at[b], sib).wait_recv()
        assemble(b)

    for ch in range(CHUNKS):
        for k in range(4):
            remote(xfin.at[ch], xfin.at[ch], az_s.at[ch, k], az_r.at[0, ch], sib).wait_send()
    flush()
    for dy in range(1, 4):
        remote(pieces.at[0], pieces.at[0], ay_s.at[dy - 1], ay_r.at[0], sib).wait_send()


G_ORDER = tuple(
    sorted(
        ((dx, dz) for dx in range(4) for dz in range(4) if dx or dz),
        key=lambda d: -(min(d[0], 4 - d[0]) + min(d[1], 4 - d[1])),
    )
)


def on_device(history, free_rows, memory_start, now):
    vmem = pltpu.VMEM
    dma = pltpu.SemaphoreType.DMA
    block = (CHUNKS, 2 * ROWS, 128)
    result = pl.pallas_call(
        kernel,
        out_shape=jax.ShapeDtypeStruct((2, 2, 256, 128), BF16),
        in_specs=[pl.BlockSpec(memory_space=pltpu.HBM)] * 4,
        out_specs=pl.BlockSpec(memory_space=pltpu.VMEM),
        scratch_shapes=[
            pltpu.SMEM((2,), jnp.int32),
            pltpu.SMEM((1,), jnp.int32),
            vmem((2, 4, 256, 128), BF16),
            vmem((4, 2, 256, 128), F32),
            vmem((4, 2, 512, 512), BF16),
            vmem((2, 2, 256, 128), BF16),
            vmem((2, 2, 64, 128), F32),
            vmem((2, 2, *block), BF16),
            vmem(block, BF16),
            vmem(block, BF16),
            vmem((ITERS, *block), BF16),
            vmem((ITERS, CHUNKS, 4, 4, *block[1:]), BF16),
            vmem((CHUNKS, 4, 4, *block[1:]), BF16),
            vmem((ITERS, CHUNKS, 4, *block[1:]), BF16),
            vmem((ITERS, CHUNKS, 4, *block[1:]), BF16),
            vmem(block, BF16),
            vmem((4, 2, CHUNKS, 2, *block[1:]), BF16),
            vmem((2, 2, 256, 128), F32),
            dma((4,)),
            dma((12,)), dma((12,)),
            dma((16,)), dma((16,)),
            dma((6,)), dma((2,)),
            dma((ITERS, CHUNKS)), dma((ITERS, CHUNKS, 4)),
            dma((CHUNKS,)), dma((CHUNKS,)),
            dma((ITERS, CHUNKS, 4)), dma((ITERS, CHUNKS)),
            dma((CHUNKS, 4)), dma((2, CHUNKS)),
            dma((3,)), dma((4,)),
            pltpu.SemaphoreType.REGULAR((5,)),
        ],
        compiler_params=pltpu.CompilerParams(
            collective_id=0, has_side_effects=True, vmem_limit_bytes=VMEM_KIB * 1024
        ),
        name="fixed_point",
    )(
        *(
            pltpu.with_memory_space_constraint(array, pltpu.HBM)
            for array in (history.reshape(2, 4, 256, 128), free_rows.reshape(2, 2, 256, 128), memory_start)
        ),
        now,
    )
    return result.reshape(free_rows.shape)


def solution(mesh):
    return jax.shard_map(
        on_device,
        mesh=mesh,
        in_specs=(P(None, "mem", None, "tt", None), P(None, None, None, "tt", None), P(), P()),
        out_specs=P(None, None, None, "tt", None),
        check_vma=False,
    )
```
